256 devices in a mesh: band: 8 (over x, core), dom: 32 (over z, y).
Axes of the slice: x: 4, y: 4, z: 8, core: 2. Of those that a mesh axis runs over, the one named last changes fastest.
Arguments:
- orbitals: float32 [64, 256, 16, 128], P('band', 'dom'), may hold values from -16 to 16
- potential: float32 [256, 16, 128], P('dom'), may hold values from -10 to 2
Outputs:
- filtered: float32 [64, 256, 16, 128], P('band', 'dom')
- hamiltonian: float32 [64, 64], P('band')
- margin: float32 [64, 64], P('band')
The draws below stay inside these ranges and needn't reach their ends.
All inputs are finite; a program needn't handle non-finite values.
Results may differ from the reference program's by a relative error of at most 0.000077.
Values sent between devices are 32-bit elements; how exact they have to be, the bound alone decides.
A program may use at most 128 MiB of HBM per device.

```python
import math
import jax
import jax.numpy as jnp
from jax import lax

ORB = 64
GX = 16
GY = 128
NZ = 256
NCELLS = 524288


def draw_orbitals(key, part):
    key = jax.random.fold_in(key, 11)
    key_base = jax.random.fold_in(key, 0)
    key_field = jax.random.fold_in(key, 2)
    key_coef = jax.random.fold_in(key, 3)
    shape_all = (ORB, NZ, GX, GY)
    shared_count = 8
    field_shape = (shared_count, NZ, GX, GY)
    coefs = jax.random.truncated_normal(key_coef, -2.5, 2.5, (ORB, shared_count), jnp.float32) * (1.5 / math.sqrt(8.0))
    base_draw = jax.random.truncated_normal(key_base, -4.0, 4.0, shape_all, jnp.float32)
    fields = jax.random.truncated_normal(key_field, -4.0, 4.0, field_shape, jnp.float32)
    mixed_draw = base_draw + 0.5 * jnp.roll(base_draw, 1, 0)
    for member in range(shared_count):
        mixed_draw = mixed_draw + coefs[:, member].reshape(ORB, 1, 1, 1) * fields[member][None]
    depth_ramp = 0.5 + jnp.arange(NZ, dtype=jnp.float32).reshape(1, NZ, 1, 1) / NZ
    return jnp.clip(mixed_draw * depth_ramp, -16.0, 16.0).astype(jnp.float32)


def levels(rng, dims, shards, low, high):
    level, own = 1.0, jax.random.fold_in(rng, 6)
    for dim, parts in shards:
        steps = jnp.exp(jax.random.uniform(jax.random.fold_in(own, dim), (parts,), jnp.float32, low / len(shards), high / len(shards)))
        level = level * jnp.repeat(steps, dims[dim] // parts).reshape([-1 if axis == dim else 1 for axis in range(len(dims))])
    return level


def setup_inputs(seed: int = 0) -> dict:
    keys = jax.random.split(jax.random.key(seed), 3)
    return {
        "orbitals": draw_orbitals(jax.random.fold_in(keys[2], 71), 0),
        "potential": jnp.clip(-10.0 + 12.0 * jax.random.uniform(keys[1], (NZ, GX, GY), jnp.float32) ** levels(keys[1], (NZ, GX, GY), ((0, 32),), -0.2, 0.2), -10.0, 2.0),
    }


stencil_weights = (-5369.0 / 1800.0, 12.0 / 7.0, -15.0 / 56.0, 10.0 / 189.0, -1.0 / 112.0, 2.0 / 825.0, -1.0 / 2772.0)
spacing = 0.35
kinetic = -0.5 / (spacing * spacing)
upper_bound = 90.0
cutoff = 8.0
lower_bound = -11.0
center = (upper_bound + cutoff) / 2.0
half_width = (upper_bound - cutoff) / 2.0
first_ratio = half_width / (lower_bound - center)
second_ratio = 1.0 / (2.0 / first_ratio - first_ratio)


def hamilton(grid_values, potential):
    summed = 3.0 * stencil_weights[0] * grid_values
    for offset in range(1, 7):
        for dimension in range(3):
            summed = summed + stencil_weights[offset] * (jnp.roll(grid_values, offset, dimension) + jnp.roll(grid_values, -offset, dimension))
    return kinetic * summed + potential * grid_values


def filter_one(orbital_block, potential):
    first_term = (hamilton(orbital_block, potential) - center * orbital_block) * (first_ratio / half_width)
    second = (2.0 * second_ratio / half_width) * (hamilton(first_term, potential) - center * first_term) - first_ratio * second_ratio * orbital_block
    return second, hamilton(second, potential)


def reference(orbitals, potential):
    filtered, applied = lax.map(lambda orbital_block: filter_one(orbital_block, potential), orbitals)
    filtered_flat = filtered.reshape(ORB, NCELLS)
    applied_flat = applied.reshape(ORB, NCELLS)
    margin = jnp.dot(filtered_flat, filtered_flat.T, precision=lax.Precision.HIGHEST, preferred_element_type=jnp.float32) / NCELLS
    hamiltonian = jnp.dot(applied_flat, filtered_flat.T, precision=lax.Precision.HIGHEST, preferred_element_type=jnp.float32) / NCELLS
    return filtered, hamiltonian, margin
```

```python
import jax
import jax.numpy as jnp
from jax import lax
from jax.experimental import pallas as pl
from jax.experimental.pallas import tpu as pltpu
from jax.sharding import PartitionSpec as P

MESH = pl.DeviceIdType.MESH

stencil_weights = (
    -5369.0 / 1800.0,
    12.0 / 7.0,
    -15.0 / 56.0,
    10.0 / 189.0,
    -1.0 / 112.0,
    2.0 / 825.0,
    -1.0 / 2772.0,
)
spacing = 0.35
kinetic = -0.5 / (spacing * spacing)
upper_bound = 90.0
cutoff = 8.0
lower_bound = -11.0
center = (upper_bound + cutoff) / 2.0
half_width = (upper_bound - cutoff) / 2.0
first_ratio = half_width / (lower_bound - center)
second_ratio = 1.0 / (2.0 / first_ratio - first_ratio)
first_scale = first_ratio / half_width
second_scale = 2.0 * second_ratio / half_width

NB = 8
NY = 4
NZ = 8
ORB = 8
LAYERS = 8
REACH = 6
TOTAL = 256 * 16 * 128


def full_stencil(pad, k, potential, scale):
    layer = [pad[k, z] for z in range(LAYERS + 2 * REACH)]
    out = []
    for z in range(LAYERS):
        mid = layer[z + REACH]
        diagonal = scale * (potential[z] + (3.0 * kinetic * stencil_weights[0] - center))
        total = diagonal * mid
        for o in range(1, REACH + 1):
            pair = layer[z + REACH + o] + layer[z + REACH - o]
            pair = pair + (pltpu.roll(mid, o, 1) + pltpu.roll(mid, 128 - o, 1))
            pair = pair + (pltpu.roll(mid, o, 0) + pltpu.roll(mid, 16 - o, 0))
            total = total + (scale * kinetic * stencil_weights[o]) * pair
        out.append(total)
    return out


def half_stencil(pad, k, potential):
    low = [pad[k, z, 8:16] for z in range(LAYERS + REACH)]
    high = [pad[k, REACH + z, 0:8] for z in range(LAYERS + REACH)]
    out = []
    for z in range(LAYERS):
        mid = pad[k, REACH + z]
        total = (0.5 * potential[z] + 1.5 * kinetic * stencil_weights[0]) * mid
        for o in range(1, REACH + 1):
            side = jnp.concatenate([high[z + o], low[z + REACH - o]], axis=0)
            pair = side + (pltpu.roll(mid, o, 1) + pltpu.roll(mid, o, 0))
            total = total + (kinetic * stencil_weights[o]) * pair
        out.append(total)
    return out


def kernel(
    orb_hbm, pot_ref, out_hbm, rows_ref,
    o_pad, u_pad, f_pad, g_buf, f_all, g_all, part, from_band, from_y, from_z,
    load_sem, store_sem,
    send1, recv1, send2, recv2, send3, recv3,
    f_send, f_recv, g_send, g_recv, r_send, r_recv,
):
    band = lax.axis_index("band")
    dom = lax.axis_index("dom")
    up = lax.rem(dom + 1, NY * NZ)
    down = lax.rem(dom + NY * NZ - 1, NY * NZ)
    y = lax.rem(dom, NY)
    z = lax.div(dom, NY)
    band_peers = [lax.rem(band + j, NB) for j in range(1, NB)]
    y_peers = [z * NY + lax.rem(y + j, NY) for j in range(1, NY)]
    z_peers = [lax.rem(z + j, NZ) * NY + y for j in range(1, NZ)]

    load = pltpu.make_async_copy(orb_hbm, o_pad.at[:, REACH : REACH + LAYERS], load_sem)
    load.start()

    barrier = pltpu.get_barrier_semaphore()
    for peer in [up, down] + y_peers + z_peers:
        pl.semaphore_signal(barrier, inc=1, device_id={"dom": peer}, device_id_type=MESH)
    for peer in band_peers:
        pl.semaphore_signal(barrier, inc=1, device_id={"band": peer}, device_id_type=MESH)
    pl.semaphore_wait(barrier, 2 + (NY - 1) + (NZ - 1) + (NB - 1))

    def first_halo(k):
        return (
            pltpu.make_async_remote_copy(
                src_ref=orb_hbm.at[k, LAYERS - REACH : LAYERS],
                dst_ref=o_pad.at[k, 0:REACH],
                send_sem=send1.at[0, k], recv_sem=recv1.at[0, k],
                device_id={"dom": up}, device_id_type=MESH,
            ),
            pltpu.make_async_remote_copy(
                src_ref=orb_hbm.at[k, 0:REACH],
                dst_ref=o_pad.at[k, REACH + LAYERS :],
                send_sem=send1.at[1, k], recv_sem=recv1.at[1, k],
                device_id={"dom": down}, device_id_type=MESH,
            ),
        )

    def second_halo(k):
        return (
            pltpu.make_async_remote_copy(
                src_ref=u_pad.at[k, LAYERS : REACH + LAYERS],
                dst_ref=u_pad.at[k, 0:REACH],
                send_sem=send2.at[0, k], recv_sem=recv2.at[0, k],
                device_id={"dom": up}, device_id_type=MESH,
            ),
            pltpu.make_async_remote_copy(
                src_ref=u_pad.at[k, REACH : 2 * REACH],
                dst_ref=u_pad.at[k, REACH + LAYERS :],
                send_sem=send2.at[1, k], recv_sem=recv2.at[1, k],
                device_id={"dom": down}, device_id_type=MESH,
            ),
        )

    def third_halo(k):
        return (
            pltpu.make_async_remote_copy(
                src_ref=f_pad.at[k, LAYERS : REACH + LAYERS, 8:16],
                dst_ref=f_pad.at[k, 0:REACH, 8:16],
                send_sem=send3.at[0, k], recv_sem=recv3.at[0, k],
                device_id={"dom": up}, device_id_type=MESH,
            ),
            pltpu.make_async_remote_copy(
                src_ref=f_pad.at[k, REACH : 2 * REACH, 0:8],
                dst_ref=f_pad.at[k, REACH + LAYERS :, 0:8],
                send_sem=send3.at[1, k], recv_sem=recv3.at[1, k],
                device_id={"dom": down}, device_id_type=MESH,
            ),
        )

    def f_share(k, peer):
        return pltpu.make_async_remote_copy(
            src_ref=f_pad.at[k, REACH + peer],
            dst_ref=f_all.at[band * ORB + k],
            send_sem=f_send, recv_sem=f_recv,
            device_id={"band": peer}, device_id_type=MESH,
        )

    def g_share(k, peer):
        return pltpu.make_async_remote_copy(
            src_ref=g_buf.at[k, peer],
            dst_ref=g_all.at[band * ORB + k],
            send_sem=g_send, recv_sem=g_recv,
            device_id={"band": peer}, device_id_type=MESH,
        )

    def store(k):
        return pltpu.make_async_copy(
            f_pad.at[k, REACH : REACH + LAYERS], out_hbm.at[k], store_sem.at[k]
        )

    @pl.loop(0, ORB)
    def _(k):
        for copy in first_halo(k):
            copy.start()

    load.wait()

    @pl.loop(0, ORB)
    def _(k):
        for copy in first_halo(k):
            copy.wait_recv()
        for layer, value in enumerate(full_stencil(o_pad, k, pot_ref, first_scale)):
            u_pad[k, REACH + layer] = value
        for copy in second_halo(k):
            copy.start()

    @pl.loop(0, ORB)
    def _(k):
        for copy in second_halo(k):
            copy.wait_recv()
        for layer, value in enumerate(full_stencil(u_pad, k, pot_ref, second_scale)):
            f_pad[k, REACH + layer] = value - (first_ratio * second_ratio) * o_pad[k, REACH + layer]
        for copy in third_halo(k):
            copy.start()
        for peer in band_peers:
            f_share(k, peer).start()
        store(k).start()
        f_all[band * ORB + k] = f_pad[k, REACH + band]

    @pl.loop(0, ORB)
    def _(k):
        for copy in third_halo(k):
            copy.wait_recv()
        for layer, value in enumerate(half_stencil(f_pad, k, pot_ref)):
            g_buf[k, layer] = value
        for peer in band_peers:
            g_share(k, peer).start()
        g_all[band * ORB + k] = g_buf[k, band]

    others = (NB - 1) * ORB
    pltpu.make_async_copy(f_all.at[0:others], f_all.at[0:others], f_recv).wait()
    pltpu.make_async_copy(g_all.at[0:others], g_all.at[0:others], g_recv).wait()

    f_rows = f_all.reshape(NB * ORB * 16, 128)
    g_rows = g_all.reshape(NB * ORB * 16, 128)
    gram = jnp.zeros((128, 128), jnp.float32)
    for r in range(0, 16, 2):
        pieces = []
        for rows in (f_rows, g_rows):
            pieces.append(
                jnp.concatenate(
                    [rows[pl.ds(r + i, NB * ORB, stride=16), :] for i in range(2)], axis=1
                )
            )
        both = jnp.concatenate(pieces, axis=0)
        gram = gram + lax.dot_general(
            both, both, (((1,), (1,)), ((), ())),
            precision=lax.Precision.HIGHEST, preferred_element_type=jnp.float32,
        )
    lane = lax.broadcasted_iota(jnp.int32, (64, 128), 1)
    flipped = pltpu.roll(gram[64:128], 64, 1)
    part[...] = (gram[0:64] + jnp.where(lane < 64, 0.0, flipped)).reshape(NB, 8, 128)

    def band_sum(peer):
        return pltpu.make_async_remote_copy(
            src_ref=part.at[peer], dst_ref=from_band.at[band],
            send_sem=r_send.at[0], recv_sem=r_recv.at[0],
            device_id={"band": peer}, device_id_type=MESH,
        )

    def y_sum(peer):
        return pltpu.make_async_remote_copy(
            src_ref=from_y.at[y], dst_ref=from_y.at[y],
            send_sem=r_send.at[1], recv_sem=r_recv.at[1],
            device_id={"dom": peer}, device_id_type=MESH,
        )

    def z_sum(peer):
        return pltpu.make_async_remote_copy(
            src_ref=from_z.at[z], dst_ref=from_z.at[z],
            send_sem=r_send.at[2], recv_sem=r_recv.at[2],
            device_id={"dom": peer}, device_id_type=MESH,
        )

    def total_of(slots, count):
        total = slots[0]
        for i in range(1, count):
            total = total + slots[i]
        return total

    for peer in band_peers:
        band_sum(peer).start()
    from_band[band] = part[band]
    pltpu.make_async_copy(
        from_band.at[0 : NB - 1], from_band.at[0 : NB - 1], r_recv.at[0]
    ).wait()
    from_y[y] = total_of(from_band, NB)
    for peer in y_peers:
        y_sum(peer).start()
    pltpu.make_async_copy(from_y.at[0 : NY - 1], from_y.at[0 : NY - 1], r_recv.at[1]).wait()
    from_z[z] = total_of(from_y, NY)
    for peer in z_peers:
        z_sum(peer).start()
    pltpu.make_async_copy(from_z.at[0 : NZ - 1], from_z.at[0 : NZ - 1], r_recv.at[2]).wait()
    rows_ref[...] = total_of(from_z, NZ) * (1.0 / TOTAL)

    @pl.loop(0, ORB)
    def _(k):
        for copy in first_halo(k) + second_halo(k) + third_halo(k):
            copy.wait_send()
        store(k).wait()

    pltpu.make_async_copy(f_all.at[0:others], f_all.at[0:others], f_send).wait()
    pltpu.make_async_copy(g_all.at[0:others], g_all.at[0:others], g_send).wait()
    for i, count in enumerate((NB - 1, NY - 1, NZ - 1)):
        pltpu.make_async_copy(from_z.at[0:count], from_z.at[0:count], r_send.at[i]).wait()


def on_device(orbitals, potential):
    f32 = jnp.float32
    dma = pltpu.SemaphoreType.DMA
    pad = pltpu.VMEM((ORB, LAYERS + 2 * REACH, 16, 128), f32)
    filtered, rows = pl.pallas_call(
        kernel,
        out_shape=(
            jax.ShapeDtypeStruct((ORB, LAYERS, 16, 128), f32),
            jax.ShapeDtypeStruct((8, 128), f32),
        ),
        in_specs=[
            pl.BlockSpec(memory_space=pl.ANY),
            pl.BlockSpec(memory_space=pltpu.VMEM),
        ],
        out_specs=(
            pl.BlockSpec(memory_space=pl.ANY),
            pl.BlockSpec(memory_space=pltpu.VMEM),
        ),
        scratch_shapes=[
            pad, pad, pad,
            pltpu.VMEM((ORB, LAYERS, 16, 128), f32),
            pltpu.VMEM((NB * ORB, 16, 128), f32),
            pltpu.VMEM((NB * ORB, 16, 128), f32),
            pltpu.VMEM((NB, 8, 128), f32),
            pltpu.VMEM((NB, 8, 128), f32),
            pltpu.VMEM((NY, 8, 128), f32),
            pltpu.VMEM((NZ, 8, 128), f32),
            dma, dma((ORB,)),
            dma((2, ORB)), dma((2, ORB)), dma((2, ORB)), dma((2, ORB)), dma((2, ORB)), dma((2, ORB)),
            dma, dma, dma, dma, dma((3,)), dma((3,)),
        ],
        compiler_params=pltpu.CompilerParams(
            collective_id=0, has_side_effects=True, vmem_limit_bytes=32 * 1024 * 1024
        ),
    )(orbitals, potential)
    return filtered, rows[:, 64:], rows[:, :64]


def solution(mesh):
    in_specs = (P("band", "dom", None, None), P("dom", None, None))
    out_specs = (P("band", "dom", None, None), P("band", None), P("band", None))
    return jax.shard_map(
        on_device, mesh=mesh, in_specs=in_specs, out_specs=out_specs, check_vma=False
    )
```

```python
import jax
import jax.numpy as jnp
from jax import lax
from jax.experimental import pallas as pl
from jax.experimental.pallas import tpu as pltpu
from jax.sharding import PartitionSpec as P

MESH = pl.DeviceIdType.MESH

stencil_weights = (
    -5369.0 / 1800.0,
    12.0 / 7.0,
    -15.0 / 56.0,
    10.0 / 189.0,
    -1.0 / 112.0,
    2.0 / 825.0,
    -1.0 / 2772.0,
)
spacing = 0.35
kinetic = -0.5 / (spacing * spacing)
upper_bound = 90.0
cutoff = 8.0
lower_bound = -11.0
center = (upper_bound + cutoff) / 2.0
half_width = (upper_bound - cutoff) / 2.0
first_ratio = half_width / (lower_bound - center)
second_ratio = 1.0 / (2.0 / first_ratio - first_ratio)
first_scale = first_ratio / half_width
second_scale = 2.0 * second_ratio / half_width

NB = 8
NY = 4
NZ = 8
ORB = 8
LAYERS = 8
REACH = 6
TOTAL = 256 * 16 * 128


def full_stencil(pad, k, potential, scale):
    layer = [pad[k, z] for z in range(LAYERS + 2 * REACH)]
    out = []
    for z in range(LAYERS):
        mid = layer[z + REACH]
        diagonal = scale * (potential[z] + (3.0 * kinetic * stencil_weights[0] - center))
        total = diagonal * mid
        for o in range(1, REACH + 1):
            pair = layer[z + REACH + o] + layer[z + REACH - o]
            pair = pair + (pltpu.roll(mid, o, 1) + pltpu.roll(mid, 128 - o, 1))
            pair = pair + (pltpu.roll(mid, o, 0) + pltpu.roll(mid, 16 - o, 0))
            total = total + (scale * kinetic * stencil_weights[o]) * pair
        out.append(total)
    return out


def half_stencil(pad, k, potential):
    low = [pad[k, z, 8:16] for z in range(LAYERS + REACH)]
    high = [pad[k, REACH + z, 0:8] for z in range(LAYERS + REACH)]
    out = []
    for z in range(LAYERS):
        mid = pad[k, REACH + z]
        total = (0.5 * potential[z] + 1.5 * kinetic * stencil_weights[0]) * mid
        for o in range(1, REACH + 1):
            side = jnp.concatenate([high[z + o], low[z + REACH - o]], axis=0)
            pair = side + (pltpu.roll(mid, o, 1) + pltpu.roll(mid, o, 0))
            total = total + (kinetic * stencil_weights[o]) * pair
        out.append(total)
    return out


def kernel(
    orb_hbm, pot_hbm, f_ref, rows_ref,
    pot_ref, o_pad, u_pad, f_pad, g_buf, f_all, g_all, part, from_band, from_y, from_z,
    load_sem,
    send1, recv1, send2, recv2, send3, recv3,
    f_send, f_recv, g_send, g_recv, r_send, r_recv,
):
    band = lax.axis_index("band")
    dom = lax.axis_index("dom")
    up = lax.rem(dom + 1, NY * NZ)
    down = lax.rem(dom + NY * NZ - 1, NY * NZ)
    y = lax.rem(dom, NY)
    z = lax.div(dom, NY)
    band_peers = [lax.rem(band + j, NB) for j in range(1, NB)]
    y_peers = [z * NY + lax.rem(y + j, NY) for j in range(1, NY)]
    z_peers = [lax.rem(z + j, NZ) * NY + y for j in range(1, NZ)]

    barrier = pltpu.get_barrier_semaphore()
    for peer in [up, down] + y_peers + z_peers:
        pl.semaphore_signal(barrier, inc=1, device_id={"dom": peer}, device_id_type=MESH)
    for peer in band_peers:
        pl.semaphore_signal(barrier, inc=1, device_id={"band": peer}, device_id_type=MESH)
    load = pltpu.make_async_copy(orb_hbm, o_pad.at[:, REACH : REACH + LAYERS], load_sem.at[0])
    load.start()
    load_pot = pltpu.make_async_copy(pot_hbm, pot_ref, load_sem.at[1])
    load_pot.start()

    pl.semaphore_wait(barrier, 2 + (NY - 1) + (NZ - 1) + (NB - 1))

    load.wait()

    def first_halo(k):
        return (
            pltpu.make_async_remote_copy(
                src_ref=o_pad.at[k, LAYERS : REACH + LAYERS],
                dst_ref=o_pad.at[k, 0:REACH],
                send_sem=send1.at[0, k], recv_sem=recv1.at[0, k],
                device_id={"dom": up}, device_id_type=MESH,
            ),
            pltpu.make_async_remote_copy(
                src_ref=o_pad.at[k, REACH : 2 * REACH],
                dst_ref=o_pad.at[k, REACH + LAYERS :],
                send_sem=send1.at[1, k], recv_sem=recv1.at[1, k],
                device_id={"dom": down}, device_id_type=MESH,
            ),
        )

    def second_halo(k):
        return (
            pltpu.make_async_remote_copy(
                src_ref=u_pad.at[k, LAYERS : REACH + LAYERS],
                dst_ref=u_pad.at[k, 0:REACH],
                send_sem=send2.at[0, k], recv_sem=recv2.at[0, k],
                device_id={"dom": up}, device_id_type=MESH,
            ),
            pltpu.make_async_remote_copy(
                src_ref=u_pad.at[k, REACH : 2 * REACH],
                dst_ref=u_pad.at[k, REACH + LAYERS :],
                send_sem=send2.at[1, k], recv_sem=recv2.at[1, k],
                device_id={"dom": down}, device_id_type=MESH,
            ),
        )

    def third_halo(k):
        return (
            pltpu.make_async_remote_copy(
                src_ref=f_pad.at[k, LAYERS : REACH + LAYERS, 8:16],
                dst_ref=f_pad.at[k, 0:REACH, 8:16],
                send_sem=send3.at[0, k], recv_sem=recv3.at[0, k],
                device_id={"dom": up}, device_id_type=MESH,
            ),
            pltpu.make_async_remote_copy(
                src_ref=f_pad.at[k, REACH : 2 * REACH, 0:8],
                dst_ref=f_pad.at[k, REACH + LAYERS :, 0:8],
                send_sem=send3.at[1, k], recv_sem=recv3.at[1, k],
                device_id={"dom": down}, device_id_type=MESH,
            ),
        )

    def f_share(k, peer):
        return pltpu.make_async_remote_copy(
            src_ref=f_pad.at[k, REACH + peer],
            dst_ref=f_all.at[band * ORB + k],
            send_sem=f_send, recv_sem=f_recv,
            device_id={"band": peer}, device_id_type=MESH,
        )

    def g_share(k, peer):
        return pltpu.make_async_remote_copy(
            src_ref=g_buf.at[k, peer],
            dst_ref=g_all.at[band * ORB + k],
            send_sem=g_send, recv_sem=g_recv,
            device_id={"band": peer}, device_id_type=MESH,
        )

    @pl.loop(0, ORB)
    def _(k):
        for copy in first_halo(k):
            copy.start()

    load_pot.wait()

    @pl.loop(0, ORB)
    def _(k):
        for copy in first_halo(k):
            copy.wait_recv()
        for layer, value in enumerate(full_stencil(o_pad, k, pot_ref, first_scale)):
            u_pad[k, REACH + layer] = value
        for copy in second_halo(k):
            copy.start()

    @pl.loop(0, ORB)
    def _(k):
        for copy in second_halo(k):
            copy.wait_recv()
        for layer, value in enumerate(full_stencil(u_pad, k, pot_ref, second_scale)):
            value = value - (first_ratio * second_ratio) * o_pad[k, REACH + layer]
            f_pad[k, REACH + layer] = value
            f_ref[k, layer] = value
        for copy in third_halo(k):
            copy.start()
        for peer in band_peers:
            f_share(k, peer).start()
        f_all[band * ORB + k] = f_pad[k, REACH + band]

    @pl.loop(0, ORB)
    def _(k):
        for copy in third_halo(k):
            copy.wait_recv()
        for layer, value in enumerate(half_stencil(f_pad, k, pot_ref)):
            g_buf[k, layer] = value
        for peer in band_peers:
            g_share(k, peer).start()
        g_all[band * ORB + k] = g_buf[k, band]

    others = (NB - 1) * ORB
    pltpu.make_async_copy(f_all.at[0:others], f_all.at[0:others], f_recv).wait()
    pltpu.make_async_copy(g_all.at[0:others], g_all.at[0:others], g_recv).wait()

    f_rows = f_all.reshape(NB * ORB * 16, 128)
    g_rows = g_all.reshape(NB * ORB * 16, 128)
    gram = jnp.zeros((128, 128), jnp.float32)
    for r in range(0, 16, 2):
        pieces = []
        for rows in (f_rows, g_rows):
            pieces.append(
                jnp.concatenate(
                    [rows[pl.ds(r + i, NB * ORB, stride=16), :] for i in range(2)], axis=1
                )
            )
        both = jnp.concatenate(pieces, axis=0)
        gram = gram + lax.dot_general(
            both, both, (((1,), (1,)), ((), ())),
            precision=lax.Precision.HIGHEST, preferred_element_type=jnp.float32,
        )
    lane = lax.broadcasted_iota(jnp.int32, (64, 128), 1)
    flipped = pltpu.roll(gram[64:128], 64, 1)
    part[...] = (gram[0:64] + jnp.where(lane < 64, 0.0, flipped)).reshape(NB, 8, 128)

    def band_sum(peer):
        return pltpu.make_async_remote_copy(
            src_ref=part.at[peer], dst_ref=from_band.at[band],
            send_sem=r_send.at[0], recv_sem=r_recv.at[0],
            device_id={"band": peer}, device_id_type=MESH,
        )

    def y_sum(peer):
        return pltpu.make_async_remote_copy(
            src_ref=from_y.at[y], dst_ref=from_y.at[y],
            send_sem=r_send.at[1], recv_sem=r_recv.at[1],
            device_id={"dom": peer}, device_id_type=MESH,
        )

    def z_sum(peer):
        return pltpu.make_async_remote_copy(
            src_ref=from_z.at[z], dst_ref=from_z.at[z],
            send_sem=r_send.at[2], recv_sem=r_recv.at[2],
            device_id={"dom": peer}, device_id_type=MESH,
        )

    def total_of(slots, count):
        total = slots[0]
        for i in range(1, count):
            total = total + slots[i]
        return total

    for peer in band_peers:
        band_sum(peer).start()
    from_band[band] = part[band]
    pltpu.make_async_copy(
        from_band.at[0 : NB - 1], from_band.at[0 : NB - 1], r_recv.at[0]
    ).wait()
    from_y[y] = total_of(from_band, NB)
    for peer in y_peers:
        y_sum(peer).start()
    pltpu.make_async_copy(from_y.at[0 : NY - 1], from_y.at[0 : NY - 1], r_recv.at[1]).wait()
    from_z[z] = total_of(from_y, NY)
    for peer in z_peers:
        z_sum(peer).start()
    pltpu.make_async_copy(from_z.at[0 : NZ - 1], from_z.at[0 : NZ - 1], r_recv.at[2]).wait()
    rows_ref[...] = total_of(from_z, NZ) * (1.0 / TOTAL)

    @pl.loop(0, ORB)
    def _(k):
        for copy in first_halo(k) + second_halo(k) + third_halo(k):
            copy.wait_send()

    pltpu.make_async_copy(f_all.at[0:others], f_all.at[0:others], f_send).wait()
    pltpu.make_async_copy(g_all.at[0:others], g_all.at[0:others], g_send).wait()
    for i, count in enumerate((NB - 1, NY - 1, NZ - 1)):
        pltpu.make_async_copy(from_z.at[0:count], from_z.at[0:count], r_send.at[i]).wait()


def finish(f_ref, rows_ref, out_hbm, ham_hbm, mar_hbm, ham, mar, sems):
    copies = [
        pltpu.make_async_copy(f_ref.at[2 * i : 2 * i + 2], out_hbm.at[2 * i : 2 * i + 2], sems.at[i])
        for i in range(4)
    ]
    copies.append(pltpu.make_async_copy(ham, ham_hbm, sems.at[4]))
    copies.append(pltpu.make_async_copy(mar, mar_hbm, sems.at[5]))
    for copy in copies[:4]:
        copy.start()
    ham[...] = rows_ref[:, 64:128]
    mar[...] = rows_ref[:, 0:64]
    for copy in copies[4:]:
        copy.start()
    for copy in copies:
        copy.wait()


def on_device(orbitals, potential):
    f32 = jnp.float32
    dma = pltpu.SemaphoreType.DMA
    pad = pltpu.VMEM((ORB, LAYERS + 2 * REACH, 16, 128), f32)
    in_hbm = pl.BlockSpec(memory_space=pltpu.HBM)
    in_vmem = pl.BlockSpec(memory_space=pltpu.VMEM)
    filtered, rows = pl.pallas_call(
        kernel,
        out_shape=(
            pltpu.VMEM((ORB, LAYERS, 16, 128), f32),
            pltpu.VMEM((8, 128), f32),
        ),
        in_specs=[in_hbm, in_hbm],
        out_specs=(in_vmem, in_vmem),
        scratch_shapes=[
            pltpu.VMEM((LAYERS, 16, 128), f32),
            pad, pad, pad,
            pltpu.VMEM((ORB, LAYERS, 16, 128), f32),
            pltpu.VMEM((NB * ORB, 16, 128), f32),
            pltpu.VMEM((NB * ORB, 16, 128), f32),
            pltpu.VMEM((NB, 8, 128), f32),
            pltpu.VMEM((NB, 8, 128), f32),
            pltpu.VMEM((NY, 8, 128), f32),
            pltpu.VMEM((NZ, 8, 128), f32),
            dma((2,)),
            dma((2, ORB)), dma((2, ORB)), dma((2, ORB)), dma((2, ORB)), dma((2, ORB)), dma((2, ORB)),
            dma, dma, dma, dma, dma((3,)), dma((3,)),
        ],
        compiler_params=pltpu.CompilerParams(
            collective_id=0, has_side_effects=True, vmem_limit_bytes=60 * 1024 * 1024
        ),
    )(orbitals, potential)
    return pl.pallas_call(
        finish,
        out_shape=(
            jax.ShapeDtypeStruct((ORB, LAYERS, 16, 128), f32),
            jax.ShapeDtypeStruct((8, 64), f32),
            jax.ShapeDtypeStruct((8, 64), f32),
        ),
        in_specs=[in_vmem, in_vmem],
        out_specs=(in_hbm, in_hbm, in_hbm),
        scratch_shapes=[pltpu.VMEM((8, 64), f32), pltpu.VMEM((8, 64), f32), dma((6,))],
        compiler_params=pltpu.CompilerParams(vmem_limit_bytes=16 * 1024 * 1024),
    )(filtered, rows)


def solution(mesh):
    in_specs = (P("band", "dom", None, None), P("dom", None, None))
    out_specs = (P("band", "dom", None, None), P("band", None), P("band", None))
    return jax.shard_map(
        on_device, mesh=mesh, in_specs=in_specs, out_specs=out_specs, check_vma=False
    )
```

```python
import jax
import jax.numpy as jnp
import ml_dtypes
import numpy as np
from jax import lax
from jax.experimental import pallas as pl
from jax.experimental.pallas import tpu as pltpu
from jax.sharding import PartitionSpec as P

MESH = pl.DeviceIdType.MESH

stencil_weights = (
    -5369.0 / 1800.0,
    12.0 / 7.0,
    -15.0 / 56.0,
    10.0 / 189.0,
    -1.0 / 112.0,
    2.0 / 825.0,
    -1.0 / 2772.0,
)
spacing = 0.35
kinetic = -0.5 / (spacing * spacing)
upper_bound = 90.0
cutoff = 8.0
lower_bound = -11.0
center = (upper_bound + cutoff) / 2.0
half_width = (upper_bound - cutoff) / 2.0
first_ratio = half_width / (lower_bound - center)
second_ratio = 1.0 / (2.0 / first_ratio - first_ratio)
first_scale = first_ratio / half_width
second_scale = 2.0 * second_ratio / half_width

NB = 8
NY = 4
NZ = 8
ORB = 8
NS = ORB // NY
LAYERS = 8
CHUNK = NY * LAYERS
REACH = 6
PLANE = NB * NY - 1
TOTAL = 256 * 16 * 128
bf16 = jnp.bfloat16
f32 = jnp.float32


def in_plane_matrices(both_sides):
    def circulant(n):
        shift = (np.arange(n)[:, None] - np.arange(n)[None, :]) % n
        matrix = np.zeros((n, n))
        for o in range(1, REACH + 1):
            matrix += stencil_weights[o] * (shift == o)
            if both_sides:
                matrix += stencil_weights[o] * (shift == n - o)
        return matrix

    def parts(matrix):
        matrix = matrix.astype(np.float32)
        high = matrix.astype(ml_dtypes.bfloat16)
        return high, (matrix - high.astype(np.float32)).astype(ml_dtypes.bfloat16)

    y_high, y_low = parts(circulant(128))
    x_high, x_low = parts(np.kron(np.eye(8), circulant(16)))
    along_y = np.block([[y_high, y_low], [y_high, np.zeros_like(y_low)]])
    return along_y, np.concatenate([x_high, x_high, x_low], axis=1)


def split(value):
    high = value.astype(bf16)
    return high, (value - high.astype(f32)).astype(bf16)


def in_plane(mid, along_y, along_x):
    high, low = split(mid.reshape(8 * 16, 128))
    y_sum = jnp.dot(jnp.concatenate([high, low], axis=1), along_y[...], preferred_element_type=f32)
    x_sum = jnp.dot(
        along_x[...], jnp.concatenate([high, low, high], axis=0), preferred_element_type=f32
    )
    return (y_sum[:, :128] + y_sum[:, 128:] + x_sum).reshape(8, 16, 128)


def full_stencil(src, first, potential, scale, along_y, along_x):
    layer = [src[first + z] for z in range(8 + 2 * REACH)]
    mid = jnp.stack(layer[REACH : REACH + 8])
    normal = []
    for z in range(REACH, REACH + 8):
        total = stencil_weights[1] * (layer[z + 1] + layer[z - 1])
        for o in range(2, REACH + 1):
            total = total + stencil_weights[o] * (layer[z + o] + layer[z - o])
        normal.append(total)
    sums = jnp.stack(normal) + in_plane(mid, along_y, along_x)
    diagonal = scale * (potential + (3.0 * kinetic * stencil_weights[0] - center))
    return (scale * kinetic) * sums + diagonal * mid


def half_stencil(src, first, potential, along_y, along_x):
    mid = src[pl.ds(first + REACH, 8)]
    above = [src[first + REACH + z, 0:8] for z in range(8 + REACH)]
    below = [src[first + z, 8:16] for z in range(8 + REACH)]
    normal = []
    for z in range(8):
        up = stencil_weights[1] * above[z + 1]
        down = stencil_weights[1] * below[z + REACH - 1]
        for o in range(2, REACH + 1):
            up = up + stencil_weights[o] * above[z + o]
            down = down + stencil_weights[o] * below[z + REACH - o]
        normal.append(jnp.concatenate([up, down], axis=0))
    sums = jnp.stack(normal) + in_plane(mid, along_y, along_x)
    return kinetic * sums + (0.5 * potential + 1.5 * kinetic * stencil_weights[0]) * mid


def kernel(
    orb_hbm, pot_hbm, mats_hbm0, mats_hbm1, mats_hbm2, mats_hbm3, f_ref, rows_ref,
    full_y, full_x, half_y, half_x,
    o_home, v_share, v_buf, o_buf, u_buf, f_buf, g_buf, f_all, g_all, f_parts, y_rows,
    part, from_band, from_y, from_z,
    load_sem, in_send, in_recv, v_send, v_recv, z_send, z_recv, h_send, h_recv,
    f_send, f_recv, g_send, g_recv, out_send, out_recv, r_send, r_recv,
):
    band = lax.axis_index("band")
    dom = lax.axis_index("dom")
    y = lax.rem(dom, NY)
    z = lax.div(dom, NY)
    z_up = lax.rem(z + 1, NZ) * NY + y
    z_down = lax.rem(z + NZ - 1, NZ) * NY + y
    y_peers = [lax.rem(y + j, NY) for j in (2, 1, 3)]

    def in_plane_peer(n):
        return lax.rem(band + lax.rem(n, NB), NB), lax.rem(y + lax.div(n, NB), NY)

    barrier = pltpu.get_barrier_semaphore()
    for j in range(1, NZ):
        pl.semaphore_signal(
            barrier, inc=1, device_id={"dom": lax.rem(z + j, NZ) * NY + y}, device_id_type=MESH
        )

    @pl.loop(1, PLANE + 1)
    def _(n):
        peer_band, peer_y = in_plane_peer(n)
        pl.semaphore_signal(
            barrier, inc=1, device_id={"band": peer_band, "dom": z * NY + peer_y}, device_id_type=MESH
        )

    loads = [
        pltpu.make_async_copy(orb_hbm, o_home, load_sem.at[0]),
        pltpu.make_async_copy(pot_hbm.at[band], v_share.at[band, y], load_sem.at[1]),
        pltpu.make_async_copy(mats_hbm0, full_y, load_sem.at[2]),
        pltpu.make_async_copy(mats_hbm1, full_x, load_sem.at[3]),
        pltpu.make_async_copy(mats_hbm2, half_y, load_sem.at[4]),
        pltpu.make_async_copy(mats_hbm3, half_x, load_sem.at[5]),
        pltpu.make_async_copy(
            orb_hbm.at[pl.ds(NS * y, NS)],
            o_buf.at[:, pl.ds(2 * REACH + LAYERS * y, LAYERS)],
            load_sem.at[6],
        ),
    ]
    for load in loads:
        load.start()
    for load in loads:
        load.wait()
    pl.semaphore_wait(barrier, PLANE + NZ - 1)

    def remote(src, dst, send, recv, where):
        return pltpu.make_async_remote_copy(
            src_ref=src, dst_ref=dst, send_sem=send, recv_sem=recv,
            device_id=where, device_id_type=MESH,
        )

    def wait_bytes(ref, sem):
        pltpu.make_async_copy(ref, ref, sem).wait()

    def in_copy(s, peer):
        return remote(
            o_home.at[NS * peer + s], o_buf.at[s, pl.ds(2 * REACH + LAYERS * y, LAYERS)],
            in_send.at[s], in_recv.at[s], {"dom": z * NY + peer},
        )

    def z_copies(src, width, send, recv):
        low, high = src.shape[0] - width, src.shape[0] - 2 * width
        return (
            remote(src.at[high:low], src.at[0:width], send.at[0], recv.at[0], {"dom": z_up}),
            remote(src.at[width : 2 * width], src.at[low:], send.at[1], recv.at[1], {"dom": z_down}),
        )

    def v_halo():
        return z_copies(v_buf, REACH, v_send.at[2], v_recv.at[2])

    def o_halo(s):
        return z_copies(o_buf.at[s], 2 * REACH, z_send.at[s], z_recv.at[s])

    def f_halo(s):
        src = f_buf.at[s]
        return (
            remote(
                src.at[CHUNK : CHUNK + REACH, 8:16], src.at[0:REACH, 8:16],
                h_send.at[s, 0], h_recv.at[s, 0], {"dom": z_up},
            ),
            remote(
                src.at[REACH : 2 * REACH, 0:8], src.at[CHUNK + REACH :, 0:8],
                h_send.at[s, 1], h_recv.at[s, 1], {"dom": z_down},
            ),
        )

    for peer in y_peers:
        remote(
            v_share.at[band, y], v_share.at[band, y], v_send.at[0, 0], v_recv.at[0, 0],
            {"dom": z * NY + peer},
        ).start()
    for s in range(NS):
        for peer in y_peers:
            in_copy(s, peer).start()
    wait_bytes(v_share.at[0, 0 : NY - 1], v_recv.at[0, 0])
    for j in range(1, NB):
        remote(
            v_share.at[band], v_share.at[band], v_send.at[1, 0], v_recv.at[1, 0],
            {"band": lax.rem(band + j, NB)},
        ).start()
    wait_bytes(o_home.at[0 : NY - 1], in_recv.at[0])
    for copy in o_halo(0):
        copy.start()
    wait_bytes(v_share.at[0 : NB - 1], v_recv.at[1, 0])
    for layer in range(CHUNK):
        v_buf[REACH + layer] = v_share[layer % NB, layer // NB]
    for copy in v_halo():
        copy.start()
    wait_bytes(o_home.at[0 : NY - 1], in_recv.at[1])
    for copy in o_halo(1):
        copy.start()
    for copy in v_halo():
        copy.wait_recv()

    def share(src, dst, s, send, recv):
        @pl.loop(1, PLANE + 1)
        def _(n):
            peer_band, peer_y = in_plane_peer(n)
            remote(
                src.at[LAYERS * peer_y + peer_band], dst.at[ORB * band + NS * y + s],
                send.at[s], recv.at[s], {"band": peer_band, "dom": z * NY + peer_y},
            ).start()

        dst[ORB * band + NS * y + s] = src[LAYERS * y + band]

    @pl.loop(0, NS)
    def _(s):
        for copy in o_halo(s):
            copy.wait_recv()
        for first in (0, 8, 16, 24, 32, 36):
            u_buf[s, first : first + 8] = full_stencil(
                o_buf.at[s], first, v_buf[first : first + 8], first_scale, full_y, full_x
            )
        for first in range(0, CHUNK, 8):
            value = full_stencil(
                u_buf.at[s], first, v_buf[REACH + first : REACH + first + 8], second_scale, full_y, full_x
            )
            old = o_buf[s, 2 * REACH + first : 2 * REACH + first + 8]
            f_buf[s, REACH + first : REACH + first + 8] = value - (first_ratio * second_ratio) * old
        for copy in f_halo(s):
            copy.start()
        share(f_buf.at[s, REACH : REACH + CHUNK], f_all, s, f_send, f_recv)

    @pl.loop(0, NS)
    def _(s):
        for copy in f_halo(s):
            copy.wait_recv()
        for first in range(0, CHUNK, 8):
            g_buf[s, first : first + 8] = half_stencil(
                f_buf.at[s], first, v_buf[REACH + first : REACH + first + 8], half_y, half_x
            )
        share(g_buf.at[s], g_all, s, g_send, g_recv)

    def out_copy(s, peer):
        return remote(
            f_buf.at[s, pl.ds(REACH + LAYERS * peer, LAYERS)], f_ref.at[NS * y + s],
            out_send, out_recv, {"dom": z * NY + peer},
        )

    for s in range(NS):
        for peer in y_peers:
            out_copy(s, peer).start()
        f_ref[NS * y + s] = f_buf[s, pl.ds(REACH + LAYERS * y, LAYERS)]

    def pieces(rows, first, count, stride, c):
        value = jnp.concatenate(
            [rows[pl.ds(first + 2 * c + i, count, stride=stride), :] for i in range(2)], axis=1
        )
        return jnp.concatenate(split(value), axis=0)

    def against_f(left, c):
        return lax.dot_general(
            left, f_parts[c], (((1,), (1,)), ((), ())), preferred_element_type=f32
        )

    f_rows = f_all.reshape(NB * ORB * 16, 128)
    g_rows = g_all.reshape(NB * ORB * 16, 128)
    for s in range(NS):
        wait_bytes(f_all.at[0:PLANE], f_recv.at[s])
    total = jnp.zeros((128, 128), f32)
    for c in range(8):
        left = pieces(f_rows, 0, 64, 16, c)
        f_parts[c] = left
        total = total + against_f(left, c)
    margin = total[0:64] + total[64:128]
    margin = margin + pltpu.roll(margin, 64, 1)
    for s in range(NS):
        wait_bytes(g_all.at[0:PLANE], g_recv.at[s])
        total = jnp.zeros((64, 128), f32)
        for c in range(8):
            total = total + against_f(pieces(g_rows, 16 * s, 32, 32, c), c)
        total = total[0:32] + total[32:64]
        y_rows[pl.ds(s, 32, stride=2), :] = total + pltpu.roll(total, 64, 1)
    one_side = y_rows[...]
    other_side = jnp.concatenate([one_side, one_side], axis=0).T
    lane = lax.broadcasted_iota(jnp.int32, (64, 128), 1)
    part[...] = jnp.where(lane < 64, margin, one_side + other_side[0:64]).reshape(NB, 8, 128)

    def total_of(slots, count):
        total = slots[0]
        for i in range(1, count):
            total = total + slots[i]
        return total

    def sum_copies():
        in_band = [
            remote(
                part.at[lax.rem(band + j, NB)], from_band.at[band], r_send.at[0], r_recv.at[0],
                {"band": lax.rem(band + j, NB)},
            )
            for j in range(1, NB)
        ]
        in_y = [
            remote(from_y.at[y], from_y.at[y], r_send.at[1], r_recv.at[1], {"dom": z * NY + peer})
            for peer in y_peers
        ]
        in_z = [
            remote(
                from_z.at[z], from_z.at[z], r_send.at[2], r_recv.at[2],
                {"dom": lax.rem(z + j, NZ) * NY + y},
            )
            for j in range(1, NZ)
        ]
        return in_band, in_y, in_z

    in_band, in_y, in_z = sum_copies()
    for copy in in_band:
        copy.start()
    from_band[band] = part[band]
    wait_bytes(from_band.at[0 : NB - 1], r_recv.at[0])
    from_y[y] = total_of(from_band, NB)
    for copy in in_y:
        copy.start()
    wait_bytes(from_y.at[0 : NY - 1], r_recv.at[1])
    from_z[z] = total_of(from_y, NY)
    for copy in in_z:
        copy.start()
    wait_bytes(from_z.at[0 : NZ - 1], r_recv.at[2])
    rows_ref[...] = total_of(from_z, NZ) * (1.0 / TOTAL)

    wait_bytes(o_home.at[0 : NS * (NY - 1)], out_recv)
    wait_bytes(o_home.at[0 : NS * (NY - 1)], out_send)
    wait_bytes(v_share.at[0, 0 : NY - 1], v_send.at[0, 0])
    wait_bytes(v_share.at[0 : NB - 1], v_send.at[1, 0])
    for copy in v_halo():
        copy.wait_send()

    @pl.loop(0, NS)
    def _(s):
        wait_bytes(o_home.at[0 : NY - 1], in_send.at[s])
        for copy in o_halo(s) + f_halo(s):
            copy.wait_send()
        wait_bytes(f_all.at[0:PLANE], f_send.at[s])
        wait_bytes(g_all.at[0:PLANE], g_send.at[s])

    for i, count in enumerate((NB - 1, NY - 1, NZ - 1)):
        wait_bytes(from_z.at[0:count], r_send.at[i])


def finish(f_ref, rows_ref, out_hbm, ham_hbm, mar_hbm, ham, mar, sems):
    copies = [
        pltpu.make_async_copy(f_ref.at[2 * i : 2 * i + 2], out_hbm.at[2 * i : 2 * i + 2], sems.at[i])
        for i in range(4)
    ]
    copies.append(pltpu.make_async_copy(ham, ham_hbm, sems.at[4]))
    copies.append(pltpu.make_async_copy(mar, mar_hbm, sems.at[5]))
    for copy in copies[:4]:
        copy.start()
    ham[...] = rows_ref[:, 64:128]
    mar[...] = rows_ref[:, 0:64]
    for copy in copies[4:]:
        copy.start()
    for copy in copies:
        copy.wait()


def on_device(orbitals, potential):
    dma = pltpu.SemaphoreType.DMA
    in_hbm = pl.BlockSpec(memory_space=pltpu.HBM)
    in_vmem = pl.BlockSpec(memory_space=pltpu.VMEM)
    matrices = [jnp.asarray(m) for both in (True, False) for m in in_plane_matrices(both)]
    filtered, rows = pl.pallas_call(
        kernel,
        out_shape=(
            pltpu.VMEM((ORB, LAYERS, 16, 128), f32),
            pltpu.VMEM((8, 128), f32),
        ),
        in_specs=[in_hbm] * 6,
        out_specs=(in_vmem, in_vmem),
        scratch_shapes=[
            pltpu.VMEM((256, 256), bf16),
            pltpu.VMEM((128, 384), bf16),
            pltpu.VMEM((256, 256), bf16),
            pltpu.VMEM((128, 384), bf16),
            pltpu.VMEM((ORB, LAYERS, 16, 128), f32),
            pltpu.VMEM((NB, NY, 16, 128), f32),
            pltpu.VMEM((CHUNK + 2 * REACH, 16, 128), f32),
            pltpu.VMEM((NS, CHUNK + 4 * REACH, 16, 128), f32),
            pltpu.VMEM((NS, CHUNK + 2 * REACH, 16, 128), f32),
            pltpu.VMEM((NS, CHUNK + 2 * REACH, 16, 128), f32),
            pltpu.VMEM((NS, CHUNK, 16, 128), f32),
            pltpu.VMEM((NB * ORB, 16, 128), f32),
            pltpu.VMEM((NB * ORB, 16, 128), f32),
            pltpu.VMEM((8, 128, 256), bf16),
            pltpu.VMEM((64, 128), f32),
            pltpu.VMEM((NB, 8, 128), f32),
            pltpu.VMEM((NB, 8, 128), f32),
            pltpu.VMEM((NY, 8, 128), f32),
            pltpu.VMEM((NZ, 8, 128), f32),
            dma((7,)),
            dma((NS,)), dma((NS,)),
            dma((3, 2)), dma((3, 2)),
            dma((NS, 2)), dma((NS, 2)),
            dma((NS, 2)), dma((NS, 2)),
            dma((NS,)), dma((NS,)), dma((NS,)), dma((NS,)),
            dma, dma, dma((3,)), dma((3,)),
        ],
        compiler_params=pltpu.CompilerParams(
            collective_id=0, has_side_effects=True, vmem_limit_bytes=60 * 1024 * 1024
        ),
    )(orbitals, potential, *matrices)
    return pl.pallas_call(
        finish,
        out_shape=(
            jax.ShapeDtypeStruct((ORB, LAYERS, 16, 128), f32),
            jax.ShapeDtypeStruct((8, 64), f32),
            jax.ShapeDtypeStruct((8, 64), f32),
        ),
        in_specs=[in_vmem, in_vmem],
        out_specs=(in_hbm, in_hbm, in_hbm),
        scratch_shapes=[pltpu.VMEM((8, 64), f32), pltpu.VMEM((8, 64), f32), dma((6,))],
        compiler_params=pltpu.CompilerParams(vmem_limit_bytes=16 * 1024 * 1024),
    )(filtered, rows)


def solution(mesh):
    in_specs = (P("band", "dom", None, None), P("dom", None, None))
    out_specs = (P("band", "dom", None, None), P("band", None), P("band", None))
    return jax.shard_map(
        on_device, mesh=mesh, in_specs=in_specs, out_specs=out_specs, check_vma=False
    )
```

```python
import jax
import jax.numpy as jnp
import ml_dtypes
import numpy as np
from jax import lax
from jax.experimental import pallas as pl
from jax.experimental.pallas import tpu as pltpu
from jax.sharding import PartitionSpec as P

MESH = pl.DeviceIdType.MESH

stencil_weights = (
    -5369.0 / 1800.0,
    12.0 / 7.0,
    -15.0 / 56.0,
    10.0 / 189.0,
    -1.0 / 112.0,
    2.0 / 825.0,
    -1.0 / 2772.0,
)
spacing = 0.35
kinetic = -0.5 / (spacing * spacing)
upper_bound = 90.0
cutoff = 8.0
lower_bound = -11.0
center = (upper_bound + cutoff) / 2.0
half_width = (upper_bound - cutoff) / 2.0
first_ratio = half_width / (lower_bound - center)
second_ratio = 1.0 / (2.0 / first_ratio - first_ratio)
first_scale = first_ratio / half_width
second_scale = 2.0 * second_ratio / half_width

NB = 8
NY = 4
NZ = 8
ORB = 8
NS = ORB // NY
LAYERS = 8
CHUNK = NY * LAYERS
REACH = 6
PLANE = NB * NY - 1
TOTAL = 256 * 16 * 128
bf16 = jnp.bfloat16
f32 = jnp.float32


def in_plane_matrices(both_sides):
    def circulant(n):
        shift = (np.arange(n)[:, None] - np.arange(n)[None, :]) % n
        matrix = np.zeros((n, n))
        for o in range(1, REACH + 1):
            matrix += stencil_weights[o] * (shift == o)
            if both_sides:
                matrix += stencil_weights[o] * (shift == n - o)
        return matrix

    def parts(matrix):
        matrix = matrix.astype(np.float32)
        high = matrix.astype(ml_dtypes.bfloat16)
        return high, (matrix - high.astype(np.float32)).astype(ml_dtypes.bfloat16)

    y_high, y_low = parts(circulant(128))
    x_high, x_low = parts(np.kron(np.eye(8), circulant(16)))
    along_y = np.block([[y_high, y_low], [y_high, np.zeros_like(y_low)]])
    return along_y, np.concatenate([x_high, x_high, x_low], axis=1)


def split(value):
    high = value.astype(bf16)
    return high, (value - high.astype(f32)).astype(bf16)


def in_plane(mid, along_y, along_x):
    high, low = split(mid.reshape(8 * 16, 128))
    y_sum = jnp.dot(jnp.concatenate([high, low], axis=1), along_y[...], preferred_element_type=f32)
    x_sum = jnp.dot(
        along_x[...], jnp.concatenate([high, low, high], axis=0), preferred_element_type=f32
    )
    return (y_sum[:, :128] + y_sum[:, 128:] + x_sum).reshape(8, 16, 128)


def full_stencil(src, first, potential, scale, along_y, along_x):
    layer = [src[first + z] for z in range(8 + 2 * REACH)]
    mid = jnp.stack(layer[REACH : REACH + 8])
    normal = []
    for z in range(REACH, REACH + 8):
        total = stencil_weights[1] * (layer[z + 1] + layer[z - 1])
        for o in range(2, REACH + 1):
            total = total + stencil_weights[o] * (layer[z + o] + layer[z - o])
        normal.append(total)
    sums = jnp.stack(normal) + in_plane(mid, along_y, along_x)
    diagonal = scale * (potential + (3.0 * kinetic * stencil_weights[0] - center))
    return (scale * kinetic) * sums + diagonal * mid


def half_stencil(src, first, potential, along_y, along_x):
    mid = src[pl.ds(first + REACH, 8)]
    above = [src[first + REACH + z, 0:8] for z in range(8 + REACH)]
    below = [src[first + z, 8:16] for z in range(8 + REACH)]
    normal = []
    for z in range(8):
        up = stencil_weights[1] * above[z + 1]
        down = stencil_weights[1] * below[z + REACH - 1]
        for o in range(2, REACH + 1):
            up = up + stencil_weights[o] * above[z + o]
            down = down + stencil_weights[o] * below[z + REACH - o]
        normal.append(jnp.concatenate([up, down], axis=0))
    sums = jnp.stack(normal) + in_plane(mid, along_y, along_x)
    return kinetic * sums + (0.5 * potential + 1.5 * kinetic * stencil_weights[0]) * mid


def kernel(
    orb_hbm, pot_hbm, mats_hbm0, mats_hbm1, mats_hbm2, mats_hbm3, f_ref, rows_ref,
    full_y, full_x, half_y, half_x,
    o_home, v_share, v_buf, o_buf, u_buf, f_buf, g_buf, f_all, g_all, f_parts, y_rows,
    m_part, m_band, m_dom, h_part, h_band, h_dom,
    load_sem, in_send, in_recv, v_send, v_recv, z_send, z_recv, h_send, h_recv,
    f_send, f_recv, g_send, g_recv, out_send, out_recv, m_send, m_recv, r_send, r_recv, relay,
):
    band = lax.axis_index("band")
    dom = lax.axis_index("dom")
    y = lax.rem(dom, NY)
    z = lax.div(dom, NY)
    z_up = lax.rem(z + 1, NZ) * NY + y
    z_down = lax.rem(z + NZ - 1, NZ) * NY + y
    y_peers = [lax.rem(y + j, NY) for j in (2, 1, 3)]
    band_peers = [lax.rem(band + j, NB) for j in (4, 3, 5, 2, 6, 1, 7)]
    z_rows = [lax.rem(z + j, NZ) * NY for j in range(NZ)]
    y_columns = [lax.rem(y + j, NY) for j in range(NY)]
    offsets = [(i, j) for i in range(NZ) for j in range(NY) if i or j]
    offsets.sort(key=lambda ij: -min(ij[0], NZ - ij[0]) - min(ij[1], NY - ij[1]))
    dom_peers = [z_rows[i] + y_columns[j] for i, j in offsets]

    def in_plane_peer(n):
        return lax.rem(band + lax.rem(n, NB), NB), lax.rem(y + lax.div(n, NB), NY)

    barrier = pltpu.get_barrier_semaphore()
    for peer in [z_up, z_down] + [z * NY + peer for peer in y_peers]:
        pl.semaphore_signal(barrier, inc=1, device_id={"dom": peer}, device_id_type=MESH)
    for peer in band_peers:
        pl.semaphore_signal(barrier, inc=1, device_id={"band": peer}, device_id_type=MESH)

    loads = [
        pltpu.make_async_copy(orb_hbm, o_home, load_sem.at[0]),
        pltpu.make_async_copy(pot_hbm.at[band], v_share.at[band, y], load_sem.at[1]),
        pltpu.make_async_copy(mats_hbm0, full_y, load_sem.at[2]),
        pltpu.make_async_copy(mats_hbm1, full_x, load_sem.at[3]),
        pltpu.make_async_copy(mats_hbm2, half_y, load_sem.at[4]),
        pltpu.make_async_copy(mats_hbm3, half_x, load_sem.at[5]),
        pltpu.make_async_copy(
            orb_hbm.at[pl.ds(NS * y, NS)],
            o_buf.at[:, pl.ds(2 * REACH + LAYERS * y, LAYERS)],
            load_sem.at[6],
        ),
    ]
    for load in loads:
        load.start()
    for load in loads:
        load.wait()
    pl.semaphore_wait(barrier, 2 + (NY - 1) + (NB - 1))

    def remote(src, dst, send, recv, where):
        return pltpu.make_async_remote_copy(
            src_ref=src, dst_ref=dst, send_sem=send, recv_sem=recv,
            device_id=where, device_id_type=MESH,
        )

    def wait_bytes(ref, sem):
        pltpu.make_async_copy(ref, ref, sem).wait()

    def in_copy(s, peer):
        return remote(
            o_home.at[NS * peer + s], o_buf.at[s, pl.ds(2 * REACH + LAYERS * y, LAYERS)],
            in_send.at[s], in_recv.at[s], {"dom": z * NY + peer},
        )

    def z_copies(src, width, send, recv):
        low, high = src.shape[0] - width, src.shape[0] - 2 * width
        return (
            remote(src.at[high:low], src.at[0:width], send.at[0], recv.at[0], {"dom": z_up}),
            remote(src.at[width : 2 * width], src.at[low:], send.at[1], recv.at[1], {"dom": z_down}),
        )

    def o_halo(s):
        return z_copies(o_buf.at[s], 2 * REACH, z_send.at[s], z_recv.at[s])

    def f_halo(s):
        src = f_buf.at[s]
        return (
            remote(
                src.at[CHUNK : CHUNK + REACH, 8:16], src.at[0:REACH, 8:16],
                h_send.at[s, 0], h_recv.at[s, 0], {"dom": z_up},
            ),
            remote(
                src.at[REACH : 2 * REACH, 0:8], src.at[CHUNK + REACH :, 0:8],
                h_send.at[s, 1], h_recv.at[s, 1], {"dom": z_down},
            ),
        )

    def v_round(slots, i):
        for peer in band_peers:
            src = v_share.at[band, slots]
            remote(src, src, v_send.at[i], v_recv.at[i], {"band": peer}).start()

    for peer in y_peers:
        src = v_share.at[band, y]
        remote(src, src, v_send.at[0], v_recv.at[0], {"dom": z * NY + peer}).start()
    for s in range(NS):
        for peer in y_peers:
            in_copy(s, peer).start()
    wait_bytes(v_share.at[0, 0 : NY - 1], v_recv.at[0])
    remote(
        v_share.at[band, NY - 1], v_share.at[band, NY], v_send.at[1], v_recv.at[1], {"dom": z_up}
    ).start()
    remote(
        v_share.at[band, 0], v_share.at[band, NY + 1], v_send.at[1], v_recv.at[1], {"dom": z_down}
    ).start()
    v_round(slice(0, NY), 2)
    wait_bytes(o_home.at[0 : NY - 1], in_recv.at[0])
    for copy in o_halo(0):
        copy.start()
    wait_bytes(v_share.at[0, 0:2], v_recv.at[1])
    v_round(slice(NY, NY + 2), 3)
    wait_bytes(v_share.at[0 : NB - 1, 0:NY], v_recv.at[2])
    for layer in range(CHUNK):
        v_buf[REACH + layer] = v_share[layer % NB, layer // NB]
    wait_bytes(o_home.at[0 : NY - 1], in_recv.at[1])
    for copy in o_halo(1):
        copy.start()

    def first_term(s, firsts):
        for first in firsts:
            u_buf[s, first : first + 8] = full_stencil(
                o_buf.at[s], first, v_buf[first : first + 8], first_scale, full_y, full_x
            )

    for s in range(NS):
        first_term(s, (12, 20))
    wait_bytes(v_share.at[0 : NB - 1, 0:2], v_recv.at[3])
    for layer in range(REACH):
        v_buf[layer] = v_share[NB - REACH + layer, NY]
        v_buf[REACH + CHUNK + layer] = v_share[layer, NY + 1]

    def share(src, dst, s, send, recv):
        @pl.loop(1, PLANE + 1)
        def _(n):
            peer_band, peer_y = in_plane_peer(n)
            remote(
                src.at[LAYERS * peer_y + peer_band], dst.at[ORB * band + NS * y + s],
                send.at[s], recv.at[s], {"band": peer_band, "dom": z * NY + peer_y},
            ).start()

        dst[ORB * band + NS * y + s] = src[LAYERS * y + band]

    @pl.loop(0, NS)
    def _(s):
        for copy in o_halo(s):
            copy.wait_recv()
        first_term(s, (0, 4, 28, 36))
        for first in range(0, CHUNK, 8):
            value = full_stencil(
                u_buf.at[s], first, v_buf[REACH + first : REACH + first + 8], second_scale, full_y, full_x
            )
            old = o_buf[s, 2 * REACH + first : 2 * REACH + first + 8]
            f_buf[s, REACH + first : REACH + first + 8] = value - (first_ratio * second_ratio) * old
        for copy in f_halo(s):
            copy.start()
        share(f_buf.at[s, REACH : REACH + CHUNK], f_all, s, f_send, f_recv)

    @pl.loop(0, NS)
    def _(s):
        for copy in f_halo(s):
            copy.wait_recv()
        for first in range(0, CHUNK, 8):
            g_buf[s, first : first + 8] = half_stencil(
                f_buf.at[s], first, v_buf[REACH + first : REACH + first + 8], half_y, half_x
            )
        share(g_buf.at[s], g_all, s, g_send, g_recv)

    for i in range(2):
        pl.semaphore_signal(relay.at[i, 0], inc=1, device_id={"dom": z_up}, device_id_type=MESH)
        pl.semaphore_signal(relay.at[i, 1], inc=1, device_id={"dom": z_down}, device_id_type=MESH)
        for j in range(2):
            pl.semaphore_wait(relay.at[i, j], 1)

    def out_copy(s, peer):
        return remote(
            f_buf.at[s, pl.ds(REACH + LAYERS * peer, LAYERS)], f_ref.at[NS * y + s],
            out_send, out_recv, {"dom": z * NY + peer},
        )

    for s in range(NS):
        for peer in y_peers:
            out_copy(s, peer).start()
        f_ref[NS * y + s] = f_buf[s, pl.ds(REACH + LAYERS * y, LAYERS)]

    def pieces(rows, first, count, stride, c):
        value = jnp.concatenate(
            [rows[pl.ds(first + 2 * c + i, count, stride=stride), :] for i in range(2)], axis=1
        )
        return jnp.concatenate(split(value), axis=0)

    def against_f(left, c):
        return lax.dot_general(
            left, f_parts[c], (((1,), (1,)), ((), ())), preferred_element_type=f32
        )

    f_rows = f_all.reshape(NB * ORB * 16, 128)
    g_rows = g_all.reshape(NB * ORB * 16, 128)
    for s in range(NS):
        wait_bytes(f_all.at[0:PLANE], f_recv.at[s])
    total = jnp.zeros((128, 128), f32)
    for c in range(8):
        left = pieces(f_rows, 0, 64, 16, c)
        f_parts[c] = left
        total = total + against_f(left, c)
    lane = lax.broadcasted_iota(jnp.int32, (NB, 4, 128), 2)

    def band_tiles(value):
        value = value.reshape(NB, 8, 128)
        return jnp.where(lane < 64, value[:, 0:4], value[:, 4:8])

    def total_of(slots, count):
        total = slots[0]
        for i in range(1, count):
            total = total + slots[i]
        return total

    def over_band(tiles, slots, send, recv):
        for peer in band_peers:
            remote(tiles.at[peer], slots.at[band], send.at[0], recv.at[0], {"band": peer}).start()
        slots[band] = tiles[band]

    def over_dom(tiles, slots, send, recv):
        wait_bytes(tiles.at[0 : NB - 1], recv.at[0])
        slots[dom] = total_of(tiles, NB)
        for peer in dom_peers:
            remote(slots.at[dom], slots.at[dom], send.at[1], recv.at[1], {"dom": peer}).start()

    def result(slots, recv):
        wait_bytes(slots.at[0 : NY * NZ - 1], recv.at[1])
        return total_of(slots, NY * NZ) * (1.0 / TOTAL)

    margin = total[0:64] + total[64:128]
    m_part[...] = band_tiles(margin + pltpu.roll(margin, 64, 1))
    over_band(m_part, m_band, m_send, m_recv)
    for s in range(NS):
        wait_bytes(g_all.at[0:PLANE], g_recv.at[s])
        total = jnp.zeros((64, 128), f32)
        for c in range(8):
            total = total + against_f(pieces(g_rows, 16 * s, 32, 32, c), c)
        total = total[0:32] + total[32:64]
        y_rows[pl.ds(s, 32, stride=2), :] = total + pltpu.roll(total, 64, 1)
        if s == 0:
            over_dom(m_band, m_dom, m_send, m_recv)
    one_side = y_rows[...]
    other_side = jnp.concatenate([one_side, one_side], axis=0).T
    h_part[...] = band_tiles(one_side + other_side[0:64])
    over_band(h_part, h_band, r_send, r_recv)
    over_dom(h_band, h_dom, r_send, r_recv)
    margin = result(m_dom, m_recv)
    hamil = result(h_dom, r_recv)
    margin = jnp.concatenate([margin, pltpu.roll(margin, 64, 1)], axis=0)
    hamil = jnp.concatenate([pltpu.roll(hamil, 64, 1), hamil], axis=0)
    rows_ref[...] = jnp.where(lax.broadcasted_iota(jnp.int32, (8, 128), 1) < 64, margin, hamil)

    wait_bytes(o_home.at[0 : NS * (NY - 1)], out_recv)
    wait_bytes(o_home.at[0 : NS * (NY - 1)], out_send)
    wait_bytes(v_share.at[0, 0 : NY - 1], v_send.at[0])
    wait_bytes(v_share.at[0, 0:2], v_send.at[1])
    wait_bytes(v_share.at[0 : NB - 1, 0:NY], v_send.at[2])
    wait_bytes(v_share.at[0 : NB - 1, 0:2], v_send.at[3])

    @pl.loop(0, NS)
    def _(s):
        wait_bytes(o_home.at[0 : NY - 1], in_send.at[s])
        for copy in o_halo(s) + f_halo(s):
            copy.wait_send()
        wait_bytes(f_all.at[0:PLANE], f_send.at[s])
        wait_bytes(g_all.at[0:PLANE], g_send.at[s])

    for send in (m_send, r_send):
        wait_bytes(h_dom.at[0 : NB - 1], send.at[0])
        wait_bytes(h_dom.at[0 : NY * NZ - 1], send.at[1])


def finish(f_ref, rows_ref, out_hbm, ham_hbm, mar_hbm, ham, mar, sems):
    copies = [
        pltpu.make_async_copy(f_ref.at[2 * i : 2 * i + 2], out_hbm.at[2 * i : 2 * i + 2], sems.at[i])
        for i in range(4)
    ]
    copies.append(pltpu.make_async_copy(ham, ham_hbm, sems.at[4]))
    copies.append(pltpu.make_async_copy(mar, mar_hbm, sems.at[5]))
    for copy in copies[:4]:
        copy.start()
    ham[...] = rows_ref[:, 64:128]
    mar[...] = rows_ref[:, 0:64]
    for copy in copies[4:]:
        copy.start()
    for copy in copies:
        copy.wait()


def on_device(orbitals, potential):
    dma = pltpu.SemaphoreType.DMA
    in_hbm = pl.BlockSpec(memory_space=pltpu.HBM)
    in_vmem = pl.BlockSpec(memory_space=pltpu.VMEM)
    matrices = [jnp.asarray(m) for both in (True, False) for m in in_plane_matrices(both)]
    filtered, rows = pl.pallas_call(
        kernel,
        out_shape=(
            pltpu.VMEM((ORB, LAYERS, 16, 128), f32),
            pltpu.VMEM((8, 128), f32),
        ),
        in_specs=[in_hbm] * 6,
        out_specs=(in_vmem, in_vmem),
        scratch_shapes=[
            pltpu.VMEM((256, 256), bf16),
            pltpu.VMEM((128, 384), bf16),
            pltpu.VMEM((256, 256), bf16),
            pltpu.VMEM((128, 384), bf16),
            pltpu.VMEM((ORB, LAYERS, 16, 128), f32),
            pltpu.VMEM((NB, NY + 2, 16, 128), f32),
            pltpu.VMEM((CHUNK + 2 * REACH, 16, 128), f32),
            pltpu.VMEM((NS, CHUNK + 4 * REACH, 16, 128), f32),
            pltpu.VMEM((NS, CHUNK + 2 * REACH, 16, 128), f32),
            pltpu.VMEM((NS, CHUNK + 2 * REACH, 16, 128), f32),
            pltpu.VMEM((NS, CHUNK, 16, 128), f32),
            pltpu.VMEM((NB * ORB, 16, 128), f32),
            pltpu.VMEM((NB * ORB, 16, 128), f32),
            pltpu.VMEM((8, 128, 256), bf16),
            pltpu.VMEM((64, 128), f32),
            pltpu.VMEM((NB, 4, 128), f32),
            pltpu.VMEM((NB, 4, 128), f32),
            pltpu.VMEM((NY * NZ, 4, 128), f32),
            pltpu.VMEM((NB, 4, 128), f32),
            pltpu.VMEM((NB, 4, 128), f32),
            pltpu.VMEM((NY * NZ, 4, 128), f32),
            dma((7,)),
            dma((NS,)), dma((NS,)),
            dma((4,)), dma((4,)),
            dma((NS, 2)), dma((NS, 2)),
            dma((NS, 2)), dma((NS, 2)),
            dma((NS,)), dma((NS,)), dma((NS,)), dma((NS,)),
            dma, dma, dma((2,)), dma((2,)), dma((2,)), dma((2,)),
            pltpu.SemaphoreType.REGULAR((2, 2)),
        ],
        compiler_params=pltpu.CompilerParams(
            collective_id=0, has_side_effects=True, vmem_limit_bytes=60 * 1024 * 1024
        ),
    )(orbitals, potential, *matrices)
    return pl.pallas_call(
        finish,
        out_shape=(
            jax.ShapeDtypeStruct((ORB, LAYERS, 16, 128), f32),
            jax.ShapeDtypeStruct((8, 64), f32),
            jax.ShapeDtypeStruct((8, 64), f32),
        ),
        in_specs=[in_vmem, in_vmem],
        out_specs=(in_hbm, in_hbm, in_hbm),
        scratch_shapes=[pltpu.VMEM((8, 64), f32), pltpu.VMEM((8, 64), f32), dma((6,))],
        compiler_params=pltpu.CompilerParams(vmem_limit_bytes=16 * 1024 * 1024),
    )(filtered, rows)


def solution(mesh):
    in_specs = (P("band", "dom", None, None), P("dom", None, None))
    out_specs = (P("band", "dom", None, None), P("band", None), P("band", None))
    return jax.shard_map(
        on_device, mesh=mesh, in_specs=in_specs, out_specs=out_specs, check_vma=False
    )
```

```python
import jax
import jax.numpy as jnp
import ml_dtypes
import numpy as np
from jax import lax
from jax.experimental import pallas as pl
from jax.experimental.pallas import tpu as pltpu
from jax.sharding import PartitionSpec as P

MESH = pl.DeviceIdType.MESH

stencil_weights = (
    -5369.0 / 1800.0,
    12.0 / 7.0,
    -15.0 / 56.0,
    10.0 / 189.0,
    -1.0 / 112.0,
    2.0 / 825.0,
    -1.0 / 2772.0,
)
spacing = 0.35
kinetic = -0.5 / (spacing * spacing)
upper_bound = 90.0
cutoff = 8.0
lower_bound = -11.0
center = (upper_bound + cutoff) / 2.0
half_width = (upper_bound - cutoff) / 2.0
first_ratio = half_width / (lower_bound - center)
second_ratio = 1.0 / (2.0 / first_ratio - first_ratio)
first_scale = first_ratio / half_width
second_scale = 2.0 * second_ratio / half_width

NB = 8
NY = 4
NZ = 8
ORB = 8
NS = ORB // NY
LAYERS = 8
CHUNK = NY * LAYERS
REACH = 6
PLANE = NB * NY - 1
TOTAL = 256 * 16 * 128
bf16 = jnp.bfloat16
f32 = jnp.float32


def in_plane_matrices(both_sides):
    def circulant(n):
        shift = (np.arange(n)[:, None] - np.arange(n)[None, :]) % n
        matrix = np.zeros((n, n))
        for o in range(1, REACH + 1):
            matrix += stencil_weights[o] * (shift == o)
            if both_sides:
                matrix += stencil_weights[o] * (shift == n - o)
        return matrix

    def parts(matrix):
        matrix = matrix.astype(np.float32)
        high = matrix.astype(ml_dtypes.bfloat16)
        return high, (matrix - high.astype(np.float32)).astype(ml_dtypes.bfloat16)

    y_high, y_low = parts(circulant(128))
    x_high, x_low = parts(np.kron(np.eye(8), circulant(16)))
    along_y = np.block([[y_high, y_low], [y_high, np.zeros_like(y_low)]])
    return along_y, np.concatenate([x_high, x_high, x_low], axis=1)


def split(value):
    high = value.astype(bf16)
    return high, (value - high.astype(f32)).astype(bf16)


def in_plane(mid, along_y, along_x):
    high, low = split(mid.reshape(8 * 16, 128))
    y_sum = jnp.dot(jnp.concatenate([high, low], axis=1), along_y[...], preferred_element_type=f32)
    x_sum = jnp.dot(
        along_x[...], jnp.concatenate([high, low, high], axis=0), preferred_element_type=f32
    )
    return (y_sum[:, :128] + y_sum[:, 128:] + x_sum).reshape(8, 16, 128)


def full_stencil(src, first, potential, scale, along_y, along_x):
    layer = [src[first + z] for z in range(8 + 2 * REACH)]
    mid = jnp.stack(layer[REACH : REACH + 8])
    normal = []
    for z in range(REACH, REACH + 8):
        total = stencil_weights[1] * (layer[z + 1] + layer[z - 1])
        for o in range(2, REACH + 1):
            total = total + stencil_weights[o] * (layer[z + o] + layer[z - o])
        normal.append(total)
    sums = jnp.stack(normal) + in_plane(mid, along_y, along_x)
    diagonal = scale * (potential + (3.0 * kinetic * stencil_weights[0] - center))
    return (scale * kinetic) * sums + diagonal * mid


def half_stencil(src, first, potential, along_y, along_x):
    mid = src[pl.ds(first + REACH, 8)]
    above = [src[first + REACH + z, 0:8] for z in range(8 + REACH)]
    below = [src[first + z, 8:16] for z in range(8 + REACH)]
    normal = []
    for z in range(8):
        up = stencil_weights[1] * above[z + 1]
        down = stencil_weights[1] * below[z + REACH - 1]
        for o in range(2, REACH + 1):
            up = up + stencil_weights[o] * above[z + o]
            down = down + stencil_weights[o] * below[z + REACH - o]
        normal.append(jnp.concatenate([up, down], axis=0))
    sums = jnp.stack(normal) + in_plane(mid, along_y, along_x)
    return kinetic * sums + (0.5 * potential + 1.5 * kinetic * stencil_weights[0]) * mid


def kernel(
    orb_hbm, pot_hbm, mats_hbm0, mats_hbm1, mats_hbm2, mats_hbm3, f_ref, rows_ref,
    full_y, full_x, half_y, half_x,
    o_home, v_share, v_buf, o_buf, u_buf, f_buf, g_buf, f_all, g_all, f_parts, y_rows,
    m_part, m_band, m_dom, h_part, h_band, h_dom,
    load_sem, in_send, in_recv, v_send, v_recv, z_send, z_recv, h_send, h_recv,
    f_send, f_recv, g_send, g_recv, out_send, out_recv, m_send, m_recv, r_send, r_recv, relay,
):
    band = lax.axis_index("band")
    dom = lax.axis_index("dom")
    y = lax.rem(dom, NY)
    z = lax.div(dom, NY)
    z_up = lax.rem(z + 1, NZ) * NY + y
    z_down = lax.rem(z + NZ - 1, NZ) * NY + y
    y_peers = [lax.rem(y + j, NY) for j in (1, 3, 2)]
    band_peers = [lax.rem(band + j, NB) for j in (4, 3, 5, 2, 6, 1, 7)]
    z_rows = [lax.rem(z + j, NZ) * NY for j in range(NZ)]
    y_columns = [lax.rem(y + j, NY) for j in range(NY)]
    offsets = [(i, j) for i in range(NZ) for j in range(NY) if i or j]
    offsets.sort(key=lambda ij: -min(ij[0], NZ - ij[0]) - min(ij[1], NY - ij[1]))
    dom_peers = [z_rows[i] + y_columns[j] for i, j in offsets]

    band_ring = [lax.rem(band + j, NB) for j in range(NB)]
    y_layers = [LAYERS * lax.rem(y + i, NY) for i in range(NY)]
    dom_ring = [z * NY + lax.rem(y + i, NY) for i in range(NY)]

    barrier = pltpu.get_barrier_semaphore()
    for peer in [z_up, z_down] + [z * NY + peer for peer in y_peers]:
        pl.semaphore_signal(barrier, inc=1, device_id={"dom": peer}, device_id_type=MESH)
    for peer in band_peers:
        pl.semaphore_signal(barrier, inc=1, device_id={"band": peer}, device_id_type=MESH)

    loads = [
        pltpu.make_async_copy(orb_hbm, o_home, load_sem.at[0]),
        pltpu.make_async_copy(pot_hbm.at[band], v_share.at[band, y], load_sem.at[1]),
        pltpu.make_async_copy(mats_hbm0, full_y, load_sem.at[2]),
        pltpu.make_async_copy(mats_hbm1, full_x, load_sem.at[3]),
        pltpu.make_async_copy(mats_hbm2, half_y, load_sem.at[4]),
        pltpu.make_async_copy(mats_hbm3, half_x, load_sem.at[5]),
        pltpu.make_async_copy(
            orb_hbm.at[pl.ds(NS * y, NS)],
            o_buf.at[:, pl.ds(2 * REACH + LAYERS * y, LAYERS)],
            load_sem.at[6],
        ),
    ]
    for load in loads:
        load.start()
    for load in loads:
        load.wait()
    pl.semaphore_wait(barrier, 2 + (NY - 1) + (NB - 1))

    def remote(src, dst, send, recv, where):
        return pltpu.make_async_remote_copy(
            src_ref=src, dst_ref=dst, send_sem=send, recv_sem=recv,
            device_id=where, device_id_type=MESH,
        )

    def wait_bytes(ref, sem):
        pltpu.make_async_copy(ref, ref, sem).wait()

    def in_copy(s, peer):
        return remote(
            o_home.at[NS * peer + s], o_buf.at[s, pl.ds(2 * REACH + LAYERS * y, LAYERS)],
            in_send.at[s], in_recv.at[s], {"dom": z * NY + peer},
        )

    def z_copies(src, width, send, recv):
        low, high = src.shape[0] - width, src.shape[0] - 2 * width
        return (
            remote(src.at[high:low], src.at[0:width], send.at[0], recv.at[0], {"dom": z_up}),
            remote(src.at[width : 2 * width], src.at[low:], send.at[1], recv.at[1], {"dom": z_down}),
        )

    def o_halo(s):
        return z_copies(o_buf.at[s], 2 * REACH, z_send.at[s], z_recv.at[s])

    def f_halo(s):
        src = f_buf.at[s]
        return (
            remote(
                src.at[CHUNK : CHUNK + REACH, 8:16], src.at[0:REACH, 8:16],
                h_send.at[s, 0], h_recv.at[s, 0], {"dom": z_up},
            ),
            remote(
                src.at[REACH : 2 * REACH, 0:8], src.at[CHUNK + REACH :, 0:8],
                h_send.at[s, 1], h_recv.at[s, 1], {"dom": z_down},
            ),
        )

    def v_round(slots, i):
        for peer in band_peers:
            src = v_share.at[band, slots]
            remote(src, src, v_send.at[i], v_recv.at[i], {"band": peer}).start()

    for peer in y_peers:
        src = v_share.at[band, y]
        remote(src, src, v_send.at[0], v_recv.at[0], {"dom": z * NY + peer}).start()
    for peer in y_peers:
        in_copy(0, peer).start()
    wait_bytes(v_share.at[0, 0 : NY - 1], v_recv.at[0])
    for peer in y_peers:
        in_copy(1, peer).start()
    remote(
        v_share.at[band, NY - 1], v_share.at[band, NY], v_send.at[1], v_recv.at[1], {"dom": z_up}
    ).start()
    remote(
        v_share.at[band, 0], v_share.at[band, NY + 1], v_send.at[1], v_recv.at[1], {"dom": z_down}
    ).start()
    v_round(slice(0, NY), 2)
    wait_bytes(o_home.at[0 : NY - 1], in_recv.at[0])
    for copy in o_halo(0):
        copy.start()
    wait_bytes(v_share.at[0, 0:2], v_recv.at[1])
    v_round(slice(NY, NY + 2), 3)
    wait_bytes(v_share.at[0 : NB - 1, 0:NY], v_recv.at[2])
    for layer in range(CHUNK):
        v_buf[REACH + layer] = v_share[layer % NB, layer // NB]
    wait_bytes(o_home.at[0 : NY - 1], in_recv.at[1])
    for copy in o_halo(1):
        copy.start()

    def first_term(s, firsts):
        for first in firsts:
            u_buf[s, first : first + 8] = full_stencil(
                o_buf.at[s], first, v_buf[first : first + 8], first_scale, full_y, full_x
            )

    for s in range(NS):
        first_term(s, (12, 20))
    wait_bytes(v_share.at[0 : NB - 1, 0:2], v_recv.at[3])
    for layer in range(REACH):
        v_buf[layer] = v_share[NB - REACH + layer, NY]
        v_buf[REACH + CHUNK + layer] = v_share[layer, NY + 1]

    def share(src, dst, s, send, recv):
        for n in range(1, PLANE + 1):
            j, i = 13 * n % (PLANE + 1) % NB, 13 * n % (PLANE + 1) // NB
            remote(
                src.at[y_layers[i] + band_ring[j]], dst.at[ORB * band + NS * y + s],
                send.at[s], recv.at[s], {"band": band_ring[j], "dom": dom_ring[i]},
            ).start()

        dst[ORB * band + NS * y + s] = src[LAYERS * y + band]

    @pl.loop(0, NS)
    def _(s):
        for copy in o_halo(s):
            copy.wait_recv()
        first_term(s, (0, 4, 28, 36))
        for first in range(0, CHUNK, 8):
            value = full_stencil(
                u_buf.at[s], first, v_buf[REACH + first : REACH + first + 8], second_scale, full_y, full_x
            )
            old = o_buf[s, 2 * REACH + first : 2 * REACH + first + 8]
            f_buf[s, REACH + first : REACH + first + 8] = value - (first_ratio * second_ratio) * old
        for copy in f_halo(s):
            copy.start()
        share(f_buf.at[s, REACH : REACH + CHUNK], f_all, s, f_send, f_recv)

    @pl.loop(0, NS)
    def _(s):
        for copy in f_halo(s):
            copy.wait_recv()
        for first in range(0, CHUNK, 8):
            g_buf[s, first : first + 8] = half_stencil(
                f_buf.at[s], first, v_buf[REACH + first : REACH + first + 8], half_y, half_x
            )
        share(g_buf.at[s], g_all, s, g_send, g_recv)

    for i in range(2):
        pl.semaphore_signal(relay.at[i, 0], inc=1, device_id={"dom": z_up}, device_id_type=MESH)
        pl.semaphore_signal(relay.at[i, 1], inc=1, device_id={"dom": z_down}, device_id_type=MESH)
        for j in range(2):
            pl.semaphore_wait(relay.at[i, j], 1)

    def out_copy(s, peer):
        return remote(
            f_buf.at[s, pl.ds(REACH + LAYERS * peer, LAYERS)], f_ref.at[NS * y + s],
            out_send, out_recv, {"dom": z * NY + peer},
        )

    for s in range(NS):
        for peer in y_peers:
            out_copy(s, peer).start()
        f_ref[NS * y + s] = f_buf[s, pl.ds(REACH + LAYERS * y, LAYERS)]

    def pieces(rows, first, count, stride, c):
        value = jnp.concatenate(
            [rows[pl.ds(first + 2 * c + i, count, stride=stride), :] for i in range(2)], axis=1
        )
        return jnp.concatenate(split(value), axis=0)

    def against_f(left, c):
        return lax.dot_general(
            left, f_parts[c], (((1,), (1,)), ((), ())), preferred_element_type=f32
        )

    f_rows = f_all.reshape(NB * ORB * 16, 128)
    g_rows = g_all.reshape(NB * ORB * 16, 128)
    for s in range(NS):
        wait_bytes(f_all.at[0:PLANE], f_recv.at[s])
    total = jnp.zeros((128, 128), f32)
    for c in range(8):
        left = pieces(f_rows, 0, 64, 16, c)
        f_parts[c] = left
        total = total + against_f(left, c)
    lane = lax.broadcasted_iota(jnp.int32, (NB, 4, 128), 2)

    def band_tiles(value):
        value = value.reshape(NB, 8, 128)
        return jnp.where(lane < 64, value[:, 0:4], value[:, 4:8])

    def total_of(slots, count):
        total = slots[0]
        for i in range(1, count):
            total = total + slots[i]
        return total

    def over_band(tiles, slots, send, recv):
        for peer in band_peers:
            remote(tiles.at[peer], slots.at[band], send.at[0], recv.at[0], {"band": peer}).start()
        slots[band] = tiles[band]

    def over_dom(tiles, slots, send, recv):
        wait_bytes(tiles.at[0 : NB - 1], recv.at[0])
        slots[dom] = total_of(tiles, NB)
        for peer in dom_peers:
            remote(slots.at[dom], slots.at[dom], send.at[1], recv.at[1], {"dom": peer}).start()

    def result(slots, recv):
        wait_bytes(slots.at[0 : NY * NZ - 1], recv.at[1])
        return total_of(slots, NY * NZ) * (1.0 / TOTAL)

    margin = total[0:64] + total[64:128]
    m_part[...] = band_tiles(margin + pltpu.roll(margin, 64, 1))
    over_band(m_part, m_band, m_send, m_recv)
    for s in range(NS):
        wait_bytes(g_all.at[0:PLANE], g_recv.at[s])
        total = jnp.zeros((64, 128), f32)
        for c in range(8):
            total = total + against_f(pieces(g_rows, 16 * s, 32, 32, c), c)
        total = total[0:32] + total[32:64]
        y_rows[pl.ds(s, 32, stride=2), :] = total + pltpu.roll(total, 64, 1)
        if s == 0:
            over_dom(m_band, m_dom, m_send, m_recv)
    one_side = y_rows[...]
    other_side = jnp.concatenate([one_side, one_side], axis=0).T
    h_part[...] = band_tiles(one_side + other_side[0:64])
    over_band(h_part, h_band, r_send, r_recv)
    over_dom(h_band, h_dom, r_send, r_recv)
    margin = result(m_dom, m_recv)
    hamil = result(h_dom, r_recv)
    margin = jnp.concatenate([margin, pltpu.roll(margin, 64, 1)], axis=0)
    hamil = jnp.concatenate([pltpu.roll(hamil, 64, 1), hamil], axis=0)
    rows_ref[...] = jnp.where(lax.broadcasted_iota(jnp.int32, (8, 128), 1) < 64, margin, hamil)

    wait_bytes(o_home.at[0 : NS * (NY - 1)], out_recv)
    wait_bytes(o_home.at[0 : NS * (NY - 1)], out_send)
    wait_bytes(v_share.at[0, 0 : NY - 1], v_send.at[0])
    wait_bytes(v_share.at[0, 0:2], v_send.at[1])
    wait_bytes(v_share.at[0 : NB - 1, 0:NY], v_send.at[2])
    wait_bytes(v_share.at[0 : NB - 1, 0:2], v_send.at[3])

    @pl.loop(0, NS)
    def _(s):
        wait_bytes(o_home.at[0 : NY - 1], in_send.at[s])
        for copy in o_halo(s) + f_halo(s):
            copy.wait_send()
        wait_bytes(f_all.at[0:PLANE], f_send.at[s])
        wait_bytes(g_all.at[0:PLANE], g_send.at[s])

    for send in (m_send, r_send):
        wait_bytes(h_dom.at[0 : NB - 1], send.at[0])
        wait_bytes(h_dom.at[0 : NY * NZ - 1], send.at[1])


def finish(f_ref, rows_ref, out_hbm, ham_hbm, mar_hbm, ham, mar, sems):
    copies = [
        pltpu.make_async_copy(f_ref.at[2 * i : 2 * i + 2], out_hbm.at[2 * i : 2 * i + 2], sems.at[i])
        for i in range(4)
    ]
    copies.append(pltpu.make_async_copy(ham, ham_hbm, sems.at[4]))
    copies.append(pltpu.make_async_copy(mar, mar_hbm, sems.at[5]))
    for copy in copies[:4]:
        copy.start()
    ham[...] = rows_ref[:, 64:128]
    mar[...] = rows_ref[:, 0:64]
    for copy in copies[4:]:
        copy.start()
    for copy in copies:
        copy.wait()


def on_device(orbitals, potential):
    dma = pltpu.SemaphoreType.DMA
    in_hbm = pl.BlockSpec(memory_space=pltpu.HBM)
    in_vmem = pl.BlockSpec(memory_space=pltpu.VMEM)
    matrices = [jnp.asarray(m) for both in (True, False) for m in in_plane_matrices(both)]
    filtered, rows = pl.pallas_call(
        kernel,
        out_shape=(
            pltpu.VMEM((ORB, LAYERS, 16, 128), f32),
            pltpu.VMEM((8, 128), f32),
        ),
        in_specs=[in_hbm] * 6,
        out_specs=(in_vmem, in_vmem),
        scratch_shapes=[
            pltpu.VMEM((256, 256), bf16),
            pltpu.VMEM((128, 384), bf16),
            pltpu.VMEM((256, 256), bf16),
            pltpu.VMEM((128, 384), bf16),
            pltpu.VMEM((ORB, LAYERS, 16, 128), f32),
            pltpu.VMEM((NB, NY + 2, 16, 128), f32),
            pltpu.VMEM((CHUNK + 2 * REACH, 16, 128), f32),
            pltpu.VMEM((NS, CHUNK + 4 * REACH, 16, 128), f32),
            pltpu.VMEM((NS, CHUNK + 2 * REACH, 16, 128), f32),
            pltpu.VMEM((NS, CHUNK + 2 * REACH, 16, 128), f32),
            pltpu.VMEM((NS, CHUNK, 16, 128), f32),
            pltpu.VMEM((NB * ORB, 16, 128), f32),
            pltpu.VMEM((NB * ORB, 16, 128), f32),
            pltpu.VMEM((8, 128, 256), bf16),
            pltpu.VMEM((64, 128), f32),
            pltpu.VMEM((NB, 4, 128), f32),
            pltpu.VMEM((NB, 4, 128), f32),
            pltpu.VMEM((NY * NZ, 4, 128), f32),
            pltpu.VMEM((NB, 4, 128), f32),
            pltpu.VMEM((NB, 4, 128), f32),
            pltpu.VMEM((NY * NZ, 4, 128), f32),
            dma((7,)),
            dma((NS,)), dma((NS,)),
            dma((4,)), dma((4,)),
            dma((NS, 2)), dma((NS, 2)),
            dma((NS, 2)), dma((NS, 2)),
            dma((NS,)), dma((NS,)), dma((NS,)), dma((NS,)),
            dma, dma, dma((2,)), dma((2,)), dma((2,)), dma((2,)),
            pltpu.SemaphoreType.REGULAR((2, 2)),
        ],
        compiler_params=pltpu.CompilerParams(
            collective_id=0, has_side_effects=True, vmem_limit_bytes=60 * 1024 * 1024
        ),
    )(orbitals, potential, *matrices)
    return pl.pallas_call(
        finish,
        out_shape=(
            jax.ShapeDtypeStruct((ORB, LAYERS, 16, 128), f32),
            jax.ShapeDtypeStruct((8, 64), f32),
            jax.ShapeDtypeStruct((8, 64), f32),
        ),
        in_specs=[in_vmem, in_vmem],
        out_specs=(in_hbm, in_hbm, in_hbm),
        scratch_shapes=[pltpu.VMEM((8, 64), f32), pltpu.VMEM((8, 64), f32), dma((6,))],
        compiler_params=pltpu.CompilerParams(vmem_limit_bytes=16 * 1024 * 1024),
    )(filtered, rows)


def solution(mesh):
    in_specs = (P("band", "dom", None, None), P("dom", None, None))
    out_specs = (P("band", "dom", None, None), P("band", None), P("band", None))
    return jax.shard_map(
        on_device, mesh=mesh, in_specs=in_specs, out_specs=out_specs, check_vma=False
    )
```

```python
import jax
import jax.numpy as jnp
import ml_dtypes
import numpy as np
from jax import lax
from jax.experimental import pallas as pl
from jax.experimental.pallas import tpu as pltpu
from jax.sharding import PartitionSpec as P

MESH = pl.DeviceIdType.MESH

stencil_weights = (
    -5369.0 / 1800.0,
    12.0 / 7.0,
    -15.0 / 56.0,
    10.0 / 189.0,
    -1.0 / 112.0,
    2.0 / 825.0,
    -1.0 / 2772.0,
)
spacing = 0.35
kinetic = -0.5 / (spacing * spacing)
upper_bound = 90.0
cutoff = 8.0
lower_bound = -11.0
center = (upper_bound + cutoff) / 2.0
half_width = (upper_bound - cutoff) / 2.0
first_ratio = half_width / (lower_bound - center)
second_ratio = 1.0 / (2.0 / first_ratio - first_ratio)
first_scale = first_ratio / half_width
second_scale = 2.0 * second_ratio / half_width

NB = 8
NY = 4
NZ = 8
ORB = 8
NS = ORB // NY
LAYERS = 8
CHUNK = NY * LAYERS
REACH = 6
PLANE = NB * NY - 1
TOTAL = 256 * 16 * 128
bf16 = jnp.bfloat16
f32 = jnp.float32


def in_plane_matrices(both_sides):
    def circulant(n):
        shift = (np.arange(n)[:, None] - np.arange(n)[None, :]) % n
        matrix = np.zeros((n, n))
        for o in range(1, REACH + 1):
            matrix += stencil_weights[o] * (shift == o)
            if both_sides:
                matrix += stencil_weights[o] * (shift == n - o)
        return matrix

    def parts(matrix):
        matrix = matrix.astype(np.float32)
        high = matrix.astype(ml_dtypes.bfloat16)
        return high, (matrix - high.astype(np.float32)).astype(ml_dtypes.bfloat16)

    y_high, y_low = parts(circulant(128))
    x_high, x_low = parts(np.kron(np.eye(8), circulant(16)))
    along_y = np.block([[y_high, y_low], [y_high, np.zeros_like(y_low)]])
    return along_y, np.concatenate([x_high, x_high, x_low], axis=1)


def split(value):
    high = value.astype(bf16)
    return high, (value - high.astype(f32)).astype(bf16)


def in_plane(mid, along_y, along_x):
    high, low = split(mid.reshape(8 * 16, 128))
    y_sum = jnp.dot(jnp.concatenate([high, low], axis=1), along_y[...], preferred_element_type=f32)
    x_sum = jnp.dot(
        along_x[...], jnp.concatenate([high, low, high], axis=0), preferred_element_type=f32
    )
    return (y_sum[:, :128] + y_sum[:, 128:] + x_sum).reshape(8, 16, 128)


def full_stencil(src, first, potential, scale, along_y, along_x):
    layer = [src[first + z] for z in range(8 + 2 * REACH)]
    mid = jnp.stack(layer[REACH : REACH + 8])
    normal = []
    for z in range(REACH, REACH + 8):
        total = stencil_weights[1] * (layer[z + 1] + layer[z - 1])
        for o in range(2, REACH + 1):
            total = total + stencil_weights[o] * (layer[z + o] + layer[z - o])
        normal.append(total)
    sums = jnp.stack(normal) + in_plane(mid, along_y, along_x)
    diagonal = scale * (potential + (3.0 * kinetic * stencil_weights[0] - center))
    return (scale * kinetic) * sums + diagonal * mid


def half_stencil(src, first, potential, along_y, along_x):
    mid = src[pl.ds(first + REACH, 8)]
    above = [src[first + REACH + z, 0:8] for z in range(8 + REACH)]
    below = [src[first + z, 8:16] for z in range(8 + REACH)]
    normal = []
    for z in range(8):
        up = stencil_weights[1] * above[z + 1]
        down = stencil_weights[1] * below[z + REACH - 1]
        for o in range(2, REACH + 1):
            up = up + stencil_weights[o] * above[z + o]
            down = down + stencil_weights[o] * below[z + REACH - o]
        normal.append(jnp.concatenate([up, down], axis=0))
    sums = jnp.stack(normal) + in_plane(mid, along_y, along_x)
    return kinetic * sums + (0.5 * potential + 1.5 * kinetic * stencil_weights[0]) * mid


def kernel(
    orb_hbm, pot_hbm, mats_hbm0, mats_hbm1, mats_hbm2, mats_hbm3, f_ref, rows_ref,
    full_y, full_x, half_y, half_x,
    o_home, v_share, v_buf, o_buf, u_buf, f_buf, g_buf, f_all, g_all, f_parts, y_rows,
    m_part, m_band, m_dom, h_part, h_band, h_dom,
    load_sem, in_send, in_recv, v_send, v_recv, z_send, z_recv, h_send, h_recv,
    f_send, f_recv, g_send, g_recv, out_send, out_recv, m_send, m_recv, r_send, r_recv, relay,
):
    band = lax.axis_index("band")
    dom = lax.axis_index("dom")
    y = lax.rem(dom, NY)
    z = lax.div(dom, NY)
    z_up = lax.rem(z + 1, NZ) * NY + y
    z_down = lax.rem(z + NZ - 1, NZ) * NY + y
    y_peers = [lax.rem(y + j, NY) for j in (1, 3, 2)]
    band_peers = [lax.rem(band + j, NB) for j in (4, 3, 5, 2, 6, 1, 7)]

    barrier = pltpu.get_barrier_semaphore()
    for peer in [z_up, z_down] + [z * NY + peer for peer in y_peers]:
        pl.semaphore_signal(barrier, inc=1, device_id={"dom": peer}, device_id_type=MESH)
    for peer in band_peers:
        pl.semaphore_signal(barrier, inc=1, device_id={"band": peer}, device_id_type=MESH)

    loads = [
        pltpu.make_async_copy(orb_hbm, o_home, load_sem.at[0]),
        pltpu.make_async_copy(pot_hbm.at[band], v_share.at[band, y], load_sem.at[1]),
        pltpu.make_async_copy(mats_hbm0, full_y, load_sem.at[2]),
        pltpu.make_async_copy(mats_hbm1, full_x, load_sem.at[3]),
        pltpu.make_async_copy(mats_hbm2, half_y, load_sem.at[4]),
        pltpu.make_async_copy(mats_hbm3, half_x, load_sem.at[5]),
        pltpu.make_async_copy(
            orb_hbm.at[pl.ds(NS * y, NS)],
            o_buf.at[:, pl.ds(2 * REACH + LAYERS * y, LAYERS)],
            load_sem.at[6],
        ),
    ]
    for load in loads:
        load.start()
    z_rows = [lax.rem(z + j, NZ) * NY for j in range(NZ)]
    y_columns = [lax.rem(y + j, NY) for j in range(NY)]
    offsets = [(i, j) for i in range(NZ) for j in range(NY) if i or j]
    offsets.sort(key=lambda ij: -min(ij[0], NZ - ij[0]) - min(ij[1], NY - ij[1]))
    dom_peers = [z_rows[i] + y_columns[j] for i, j in offsets]

    band_ring = [lax.rem(band + j, NB) for j in range(NB)]
    y_layers = [LAYERS * lax.rem(y + i, NY) for i in range(NY)]
    dom_ring = [z * NY + lax.rem(y + i, NY) for i in range(NY)]

    for load in loads:
        load.wait()
    pl.semaphore_wait(barrier, 2 + (NY - 1) + (NB - 1))

    def remote(src, dst, send, recv, where):
        return pltpu.make_async_remote_copy(
            src_ref=src, dst_ref=dst, send_sem=send, recv_sem=recv,
            device_id=where, device_id_type=MESH,
        )

    def wait_bytes(ref, sem):
        pltpu.make_async_copy(ref, ref, sem).wait()

    def in_copy(s, peer):
        return remote(
            o_home.at[NS * peer + s], o_buf.at[s, pl.ds(2 * REACH + LAYERS * y, LAYERS)],
            in_send.at[s], in_recv.at[s], {"dom": z * NY + peer},
        )

    def z_copies(src, width, send, recv):
        low, high = src.shape[0] - width, src.shape[0] - 2 * width
        return (
            remote(src.at[high:low], src.at[0:width], send.at[0], recv.at[0], {"dom": z_up}),
            remote(src.at[width : 2 * width], src.at[low:], send.at[1], recv.at[1], {"dom": z_down}),
        )

    def o_halo(s):
        return z_copies(o_buf.at[s], 2 * REACH, z_send.at[s], z_recv.at[s])

    def f_halo(s):
        src = f_buf.at[s]
        return (
            remote(
                src.at[CHUNK : CHUNK + REACH, 8:16], src.at[0:REACH, 8:16],
                h_send.at[s, 0], h_recv.at[s, 0], {"dom": z_up},
            ),
            remote(
                src.at[REACH : 2 * REACH, 0:8], src.at[CHUNK + REACH :, 0:8],
                h_send.at[s, 1], h_recv.at[s, 1], {"dom": z_down},
            ),
        )

    def pass_on(i):
        pl.semaphore_signal(relay.at[i, 0], inc=1, device_id={"dom": z_up}, device_id_type=MESH)
        pl.semaphore_signal(relay.at[i, 1], inc=1, device_id={"dom": z_down}, device_id_type=MESH)

    def hear(i):
        for j in range(2):
            pl.semaphore_wait(relay.at[i, j], 1)

    def v_round(slots, i):
        for peer in band_peers:
            src = v_share.at[band, slots]
            remote(src, src, v_send.at[i], v_recv.at[i], {"band": peer}).start()

    for peer in y_peers:
        src = v_share.at[band, y]
        remote(src, src, v_send.at[0], v_recv.at[0], {"dom": z * NY + peer}).start()
    for peer in y_peers:
        in_copy(0, peer).start()
    wait_bytes(v_share.at[0, 0 : NY - 1], v_recv.at[0])
    for peer in y_peers:
        in_copy(1, peer).start()
    remote(
        v_share.at[band, NY - 1], v_share.at[band, NY], v_send.at[1], v_recv.at[1], {"dom": z_up}
    ).start()
    remote(
        v_share.at[band, 0], v_share.at[band, NY + 1], v_send.at[1], v_recv.at[1], {"dom": z_down}
    ).start()
    v_round(slice(0, NY), 2)
    wait_bytes(o_home.at[0 : NY - 1], in_recv.at[0])
    for copy in o_halo(0):
        copy.start()
    wait_bytes(v_share.at[0, 0:2], v_recv.at[1])
    v_round(slice(NY, NY + 2), 3)
    pass_on(0)
    wait_bytes(v_share.at[0 : NB - 1, 0:NY], v_recv.at[2])
    for layer in range(CHUNK):
        v_buf[REACH + layer] = v_share[layer % NB, layer // NB]
    wait_bytes(o_home.at[0 : NY - 1], in_recv.at[1])
    for copy in o_halo(1):
        copy.start()

    def first_term(s, firsts):
        for first in firsts:
            u_buf[s, first : first + 8] = full_stencil(
                o_buf.at[s], first, v_buf[first : first + 8], first_scale, full_y, full_x
            )

    for s in range(NS):
        first_term(s, (12, 20))
    wait_bytes(v_share.at[0 : NB - 1, 0:2], v_recv.at[3])
    for layer in range(REACH):
        v_buf[layer] = v_share[NB - REACH + layer, NY]
        v_buf[REACH + CHUNK + layer] = v_share[layer, NY + 1]

    def share_layers(i, src, dst, s, send, recv):
        slot = ORB * band + NS * y + s
        for j in (3, 6, 1, 4, 7, 2, 5, 0):
            if i or j:
                remote(
                    src.at[y_layers[i] + band_ring[j]], dst.at[slot],
                    send.at[s], recv.at[s], {"band": band_ring[j], "dom": dom_ring[i]},
                ).start()
        if i == 0:
            dst[slot] = src[LAYERS * y + band]

    hear(0)
    pass_on(1)

    @pl.loop(0, NS)
    def _(s):
        for copy in o_halo(s):
            copy.wait_recv()
        first_term(s, (0, 4, 28, 36))
        for i in (1, 3, 2, 0):
            first = y_layers[i]
            value = full_stencil(
                u_buf.at[s], first, v_buf[pl.ds(REACH + first, 8)], second_scale, full_y, full_x
            )
            old = o_buf[s, pl.ds(2 * REACH + first, 8)]
            f_buf[s, pl.ds(REACH + first, 8)] = value - (first_ratio * second_ratio) * old
            share_layers(i, f_buf.at[s, REACH : REACH + CHUNK], f_all, s, f_send, f_recv)
        for copy in f_halo(s):
            copy.start()

    hear(1)
    pass_on(2)

    @pl.loop(0, NS)
    def _(s):
        for copy in f_halo(s):
            copy.wait_recv()
        for i in (1, 3, 2, 0):
            first = y_layers[i]
            g_buf[s, pl.ds(first, 8)] = half_stencil(
                f_buf.at[s], first, v_buf[pl.ds(REACH + first, 8)], half_y, half_x
            )
            share_layers(i, g_buf.at[s], g_all, s, g_send, g_recv)

    hear(2)

    def out_copy(s, peer):
        return remote(
            f_buf.at[s, pl.ds(REACH + LAYERS * peer, LAYERS)], f_ref.at[NS * y + s],
            out_send, out_recv, {"dom": z * NY + peer},
        )

    for s in range(NS):
        for peer in y_peers:
            out_copy(s, peer).start()
        f_ref[NS * y + s] = f_buf[s, pl.ds(REACH + LAYERS * y, LAYERS)]

    def pieces(rows, first, count, stride, c):
        value = jnp.concatenate(
            [rows[pl.ds(first + 2 * c + i, count, stride=stride), :] for i in range(2)], axis=1
        )
        return jnp.concatenate(split(value), axis=0)

    def against_f(left, c):
        return lax.dot_general(
            left, f_parts[c], (((1,), (1,)), ((), ())), preferred_element_type=f32
        )

    f_rows = f_all.reshape(NB * ORB * 16, 128)
    g_rows = g_all.reshape(NB * ORB * 16, 128)
    for s in range(NS):
        wait_bytes(f_all.at[0:PLANE], f_recv.at[s])
    total = jnp.zeros((128, 128), f32)
    for c in range(8):
        left = pieces(f_rows, 0, 64, 16, c)
        f_parts[c] = left
        total = total + against_f(left, c)
    lane = lax.broadcasted_iota(jnp.int32, (NB, 4, 128), 2)

    def band_tiles(value):
        value = value.reshape(NB, 8, 128)
        return jnp.where(lane < 64, value[:, 0:4], value[:, 4:8])

    def total_of(slots, count):
        total = slots[0]
        for i in range(1, count):
            total = total + slots[i]
        return total

    def over_band(tiles, slots, send, recv):
        for peer in band_peers:
            remote(tiles.at[peer], slots.at[band], send.at[0], recv.at[0], {"band": peer}).start()
        slots[band] = tiles[band]

    def over_dom(tiles, slots, send, recv):
        wait_bytes(tiles.at[0 : NB - 1], recv.at[0])
        slots[dom] = total_of(tiles, NB)
        for peer in dom_peers:
            remote(slots.at[dom], slots.at[dom], send.at[1], recv.at[1], {"dom": peer}).start()

    def result(slots, recv):
        wait_bytes(slots.at[0 : NY * NZ - 1], recv.at[1])
        return total_of(slots, NY * NZ) * (1.0 / TOTAL)

    margin = total[0:64] + total[64:128]
    m_part[...] = band_tiles(margin + pltpu.roll(margin, 64, 1))
    over_band(m_part, m_band, m_send, m_recv)
    for s in range(NS):
        wait_bytes(g_all.at[0:PLANE], g_recv.at[s])
        total = jnp.zeros((64, 128), f32)
        for c in range(8):
            total = total + against_f(pieces(g_rows, 16 * s, 32, 32, c), c)
        total = total[0:32] + total[32:64]
        y_rows[pl.ds(s, 32, stride=2), :] = total + pltpu.roll(total, 64, 1)
        if s == 0:
            over_dom(m_band, m_dom, m_send, m_recv)
    one_side = y_rows[...]
    other_side = jnp.concatenate([one_side, one_side], axis=0).T
    h_part[...] = band_tiles(one_side + other_side[0:64])
    over_band(h_part, h_band, r_send, r_recv)
    over_dom(h_band, h_dom, r_send, r_recv)
    margin = result(m_dom, m_recv)
    hamil = result(h_dom, r_recv)
    margin = jnp.concatenate([margin, pltpu.roll(margin, 64, 1)], axis=0)
    hamil = jnp.concatenate([pltpu.roll(hamil, 64, 1), hamil], axis=0)
    rows_ref[...] = jnp.where(lax.broadcasted_iota(jnp.int32, (8, 128), 1) < 64, margin, hamil)

    wait_bytes(o_home.at[0 : NS * (NY - 1)], out_recv)
    wait_bytes(o_home.at[0 : NS * (NY - 1)], out_send)
    wait_bytes(v_share.at[0, 0 : NY - 1], v_send.at[0])
    wait_bytes(v_share.at[0, 0:2], v_send.at[1])
    wait_bytes(v_share.at[0 : NB - 1, 0:NY], v_send.at[2])
    wait_bytes(v_share.at[0 : NB - 1, 0:2], v_send.at[3])

    @pl.loop(0, NS)
    def _(s):
        wait_bytes(o_home.at[0 : NY - 1], in_send.at[s])
        for copy in o_halo(s) + f_halo(s):
            copy.wait_send()
        wait_bytes(f_all.at[0:PLANE], f_send.at[s])
        wait_bytes(g_all.at[0:PLANE], g_send.at[s])

    for send in (m_send, r_send):
        wait_bytes(h_dom.at[0 : NB - 1], send.at[0])
        wait_bytes(h_dom.at[0 : NY * NZ - 1], send.at[1])


def finish(f_ref, rows_ref, out_hbm, ham_hbm, mar_hbm, ham, mar, sems):
    copies = [
        pltpu.make_async_copy(f_ref.at[2 * i : 2 * i + 2], out_hbm.at[2 * i : 2 * i + 2], sems.at[i])
        for i in range(4)
    ]
    copies.append(pltpu.make_async_copy(ham, ham_hbm, sems.at[4]))
    copies.append(pltpu.make_async_copy(mar, mar_hbm, sems.at[5]))
    for copy in copies[:4]:
        copy.start()
    ham[...] = rows_ref[:, 64:128]
    mar[...] = rows_ref[:, 0:64]
    for copy in copies[4:]:
        copy.start()
    for copy in copies:
        copy.wait()


def on_device(orbitals, potential):
    dma = pltpu.SemaphoreType.DMA
    in_hbm = pl.BlockSpec(memory_space=pltpu.HBM)
    in_vmem = pl.BlockSpec(memory_space=pltpu.VMEM)
    matrices = [jnp.asarray(m) for both in (True, False) for m in in_plane_matrices(both)]
    filtered, rows = pl.pallas_call(
        kernel,
        out_shape=(
            pltpu.VMEM((ORB, LAYERS, 16, 128), f32),
            pltpu.VMEM((8, 128), f32),
        ),
        in_specs=[in_hbm] * 6,
        out_specs=(in_vmem, in_vmem),
        scratch_shapes=[
            pltpu.VMEM((256, 256), bf16),
            pltpu.VMEM((128, 384), bf16),
            pltpu.VMEM((256, 256), bf16),
            pltpu.VMEM((128, 384), bf16),
            pltpu.VMEM((ORB, LAYERS, 16, 128), f32),
            pltpu.VMEM((NB, NY + 2, 16, 128), f32),
            pltpu.VMEM((CHUNK + 2 * REACH, 16, 128), f32),
            pltpu.VMEM((NS, CHUNK + 4 * REACH, 16, 128), f32),
            pltpu.VMEM((NS, CHUNK + 2 * REACH, 16, 128), f32),
            pltpu.VMEM((NS, CHUNK + 2 * REACH, 16, 128), f32),
            pltpu.VMEM((NS, CHUNK, 16, 128), f32),
            pltpu.VMEM((NB * ORB, 16, 128), f32),
            pltpu.VMEM((NB * ORB, 16, 128), f32),
            pltpu.VMEM((8, 128, 256), bf16),
            pltpu.VMEM((64, 128), f32),
            pltpu.VMEM((NB, 4, 128), f32),
            pltpu.VMEM((NB, 4, 128), f32),
            pltpu.VMEM((NY * NZ, 4, 128), f32),
            pltpu.VMEM((NB, 4, 128), f32),
            pltpu.VMEM((NB, 4, 128), f32),
            pltpu.VMEM((NY * NZ, 4, 128), f32),
            dma((7,)),
            dma((NS,)), dma((NS,)),
            dma((4,)), dma((4,)),
            dma((NS, 2)), dma((NS, 2)),
            dma((NS, 2)), dma((NS, 2)),
            dma((NS,)), dma((NS,)), dma((NS,)), dma((NS,)),
            dma, dma, dma((2,)), dma((2,)), dma((2,)), dma((2,)),
            pltpu.SemaphoreType.REGULAR((3, 2)),
        ],
        compiler_params=pltpu.CompilerParams(
            collective_id=0, has_side_effects=True, vmem_limit_bytes=60 * 1024 * 1024
        ),
    )(orbitals, potential, *matrices)
    return pl.pallas_call(
        finish,
        out_shape=(
            jax.ShapeDtypeStruct((ORB, LAYERS, 16, 128), f32),
            jax.ShapeDtypeStruct((8, 64), f32),
            jax.ShapeDtypeStruct((8, 64), f32),
        ),
        in_specs=[in_vmem, in_vmem],
        out_specs=(in_hbm, in_hbm, in_hbm),
        scratch_shapes=[pltpu.VMEM((8, 64), f32), pltpu.VMEM((8, 64), f32), dma((6,))],
        compiler_params=pltpu.CompilerParams(vmem_limit_bytes=16 * 1024 * 1024),
    )(filtered, rows)


def solution(mesh):
    in_specs = (P("band", "dom", None, None), P("dom", None, None))
    out_specs = (P("band", "dom", None, None), P("band", None), P("band", None))
    return jax.shard_map(
        on_device, mesh=mesh, in_specs=in_specs, out_specs=out_specs, check_vma=False
    )
```

```python
import jax
import jax.numpy as jnp
import ml_dtypes
import numpy as np
from jax import lax
from jax.experimental import pallas as pl
from jax.experimental.pallas import tpu as pltpu
from jax.sharding import PartitionSpec as P

MESH = pl.DeviceIdType.MESH

stencil_weights = (
    -5369.0 / 1800.0,
    12.0 / 7.0,
    -15.0 / 56.0,
    10.0 / 189.0,
    -1.0 / 112.0,
    2.0 / 825.0,
    -1.0 / 2772.0,
)
spacing = 0.35
kinetic = -0.5 / (spacing * spacing)
upper_bound = 90.0
cutoff = 8.0
lower_bound = -11.0
center = (upper_bound + cutoff) / 2.0
half_width = (upper_bound - cutoff) / 2.0
first_ratio = half_width / (lower_bound - center)
second_ratio = 1.0 / (2.0 / first_ratio - first_ratio)
first_scale = first_ratio / half_width
second_scale = 2.0 * second_ratio / half_width

NB = 8
NY = 4
NZ = 8
ORB = 8
NS = ORB // NY
LAYERS = 8
CHUNK = NY * LAYERS
REACH = 6
PLANE = NB * NY - 1
TOTAL = 256 * 16 * 128
bf16 = jnp.bfloat16
f32 = jnp.float32


def in_plane_matrices(both_sides):
    def circulant(n):
        shift = (np.arange(n)[:, None] - np.arange(n)[None, :]) % n
        matrix = np.zeros((n, n))
        for o in range(1, REACH + 1):
            matrix += stencil_weights[o] * (shift == o)
            if both_sides:
                matrix += stencil_weights[o] * (shift == n - o)
        return matrix

    def parts(matrix):
        matrix = matrix.astype(np.float32)
        high = matrix.astype(ml_dtypes.bfloat16)
        return high, (matrix - high.astype(np.float32)).astype(ml_dtypes.bfloat16)

    y_high, y_low = parts(circulant(128))
    x_high, x_low = parts(np.kron(np.eye(8), circulant(16)))
    along_y = np.block([[y_high, y_low], [y_high, np.zeros_like(y_low)]])
    return along_y, np.concatenate([x_high, x_high, x_low], axis=1)


def split(value):
    high = value.astype(bf16)
    return high, (value - high.astype(f32)).astype(bf16)


def in_plane(mid, along_y, along_x):
    high, low = split(mid.reshape(8 * 16, 128))
    y_sum = jnp.dot(jnp.concatenate([high, low], axis=1), along_y[...], preferred_element_type=f32)
    x_sum = jnp.dot(
        along_x[...], jnp.concatenate([high, low, high], axis=0), preferred_element_type=f32
    )
    return (y_sum[:, :128] + y_sum[:, 128:] + x_sum).reshape(8, 16, 128)


def full_stencil(src, first, potential, scale, along_y, along_x):
    layer = [src[first + z] for z in range(8 + 2 * REACH)]
    mid = jnp.stack(layer[REACH : REACH + 8])
    normal = []
    for z in range(REACH, REACH + 8):
        total = stencil_weights[1] * (layer[z + 1] + layer[z - 1])
        for o in range(2, REACH + 1):
            total = total + stencil_weights[o] * (layer[z + o] + layer[z - o])
        normal.append(total)
    sums = jnp.stack(normal) + in_plane(mid, along_y, along_x)
    diagonal = scale * (potential + (3.0 * kinetic * stencil_weights[0] - center))
    return (scale * kinetic) * sums + diagonal * mid


def half_stencil(src, first, potential, along_y, along_x):
    mid = src[pl.ds(first + REACH, 8)]
    above = [src[first + REACH + z, 0:8] for z in range(8 + REACH)]
    below = [src[first + z, 8:16] for z in range(8 + REACH)]
    normal = []
    for z in range(8):
        up = stencil_weights[1] * above[z + 1]
        down = stencil_weights[1] * below[z + REACH - 1]
        for o in range(2, REACH + 1):
            up = up + stencil_weights[o] * above[z + o]
            down = down + stencil_weights[o] * below[z + REACH - o]
        normal.append(jnp.concatenate([up, down], axis=0))
    sums = jnp.stack(normal) + in_plane(mid, along_y, along_x)
    return kinetic * sums + (0.5 * potential + 1.5 * kinetic * stencil_weights[0]) * mid


def kernel(
    orb_hbm, pot_hbm, mats_hbm0, mats_hbm1, mats_hbm2, mats_hbm3, f_ref, rows_ref,
    full_y, full_x, half_y, half_x,
    o_home, v_share, v_buf, o_buf, u_buf, f_buf, g_buf, f_all, g_all, f_parts, y_rows,
    m_part, m_band, m_dom, h_part, h_band, h_dom,
    load_sem, in_send, in_recv, v_send, v_recv, z_send, z_recv, h_send, h_recv,
    f_send, f_recv, g_send, g_recv, out_send, out_recv, m_send, m_recv, r_send, r_recv, relay,
):
    band = lax.axis_index("band")
    dom = lax.axis_index("dom")
    y = lax.rem(dom, NY)
    z = lax.div(dom, NY)
    z_up = lax.rem(z + 1, NZ) * NY + y
    z_down = lax.rem(z + NZ - 1, NZ) * NY + y
    y_peers = [lax.rem(y + j, NY) for j in (1, 3, 2)]
    band_peers = [lax.rem(band + j, NB) for j in (4, 3, 5, 2, 6, 1, 7)]

    barrier = pltpu.get_barrier_semaphore()
    for peer in [z_up, z_down] + [z * NY + peer for peer in y_peers]:
        pl.semaphore_signal(barrier, inc=1, device_id={"dom": peer}, device_id_type=MESH)
    for peer in band_peers:
        pl.semaphore_signal(barrier, inc=1, device_id={"band": peer}, device_id_type=MESH)

    loads = [
        pltpu.make_async_copy(orb_hbm, o_home, load_sem.at[0]),
        pltpu.make_async_copy(pot_hbm.at[band], v_share.at[band, y], load_sem.at[1]),
        pltpu.make_async_copy(mats_hbm0, full_y, load_sem.at[2]),
        pltpu.make_async_copy(mats_hbm1, full_x, load_sem.at[3]),
        pltpu.make_async_copy(mats_hbm2, half_y, load_sem.at[4]),
        pltpu.make_async_copy(mats_hbm3, half_x, load_sem.at[5]),
        pltpu.make_async_copy(
            orb_hbm.at[pl.ds(NS * y, NS)],
            o_buf.at[:, pl.ds(2 * REACH + LAYERS * y, LAYERS)],
            load_sem.at[6],
        ),
    ]
    for load in loads:
        load.start()
    z_rows = [lax.rem(z + j, NZ) * NY for j in range(NZ)]
    y_columns = [lax.rem(y + j, NY) for j in range(NY)]
    offsets = [(i, j) for i in range(NZ) for j in range(NY) if i or j]
    offsets.sort(key=lambda ij: -min(ij[0], NZ - ij[0]) - min(ij[1], NY - ij[1]))
    dom_peers = [z_rows[i] + y_columns[j] for i, j in offsets]

    band_ring = [lax.rem(band + j, NB) for j in range(NB)]
    y_layers = [LAYERS * lax.rem(y + i, NY) for i in range(NY)]
    dom_ring = [z * NY + lax.rem(y + i, NY) for i in range(NY)]

    for load in loads:
        load.wait()
    pl.semaphore_wait(barrier, 2 + (NY - 1) + (NB - 1))

    def remote(src, dst, send, recv, where):
        return pltpu.make_async_remote_copy(
            src_ref=src, dst_ref=dst, send_sem=send, recv_sem=recv,
            device_id=where, device_id_type=MESH,
        )

    def wait_bytes(ref, sem):
        pltpu.make_async_copy(ref, ref, sem).wait()

    def in_copy(s, peer):
        return remote(
            o_home.at[NS * peer + s], o_buf.at[s, pl.ds(2 * REACH + LAYERS * y, LAYERS)],
            in_send.at[s], in_recv.at[s], {"dom": z * NY + peer},
        )

    def z_copies(src, width, send, recv):
        low, high = src.shape[0] - width, src.shape[0] - 2 * width
        return (
            remote(src.at[high:low], src.at[0:width], send.at[0], recv.at[0], {"dom": z_up}),
            remote(src.at[width : 2 * width], src.at[low:], send.at[1], recv.at[1], {"dom": z_down}),
        )

    def o_halo(s):
        return z_copies(o_buf.at[s], 2 * REACH, z_send.at[s], z_recv.at[s])

    def f_halo(s):
        src = f_buf.at[s]
        return (
            remote(
                src.at[CHUNK : CHUNK + REACH, 8:16], src.at[0:REACH, 8:16],
                h_send.at[s, 0], h_recv.at[s, 0], {"dom": z_up},
            ),
            remote(
                src.at[REACH : 2 * REACH, 0:8], src.at[CHUNK + REACH :, 0:8],
                h_send.at[s, 1], h_recv.at[s, 1], {"dom": z_down},
            ),
        )

    def pass_on(i):
        pl.semaphore_signal(relay.at[i, 0], inc=1, device_id={"dom": z_up}, device_id_type=MESH)
        pl.semaphore_signal(relay.at[i, 1], inc=1, device_id={"dom": z_down}, device_id_type=MESH)

    def hear(i):
        for j in range(2):
            pl.semaphore_wait(relay.at[i, j], 1)

    def v_round(slots, i):
        for peer in band_peers:
            src = v_share.at[band, slots]
            remote(src, src, v_send.at[i], v_recv.at[i], {"band": peer}).start()

    for peer in y_peers:
        src = v_share.at[band, y]
        remote(src, src, v_send.at[0], v_recv.at[0], {"dom": z * NY + peer}).start()
    for peer in y_peers:
        in_copy(0, peer).start()
    wait_bytes(v_share.at[0, 0 : NY - 1], v_recv.at[0])
    for peer in y_peers:
        in_copy(1, peer).start()
    remote(
        v_share.at[band, NY - 1], v_share.at[band, NY], v_send.at[1], v_recv.at[1], {"dom": z_up}
    ).start()
    remote(
        v_share.at[band, 0], v_share.at[band, NY + 1], v_send.at[1], v_recv.at[1], {"dom": z_down}
    ).start()
    v_round(slice(0, NY), 2)
    wait_bytes(o_home.at[0 : NY - 1], in_recv.at[0])
    for copy in o_halo(0):
        copy.start()
    wait_bytes(v_share.at[0, 0:2], v_recv.at[1])
    v_round(slice(NY, NY + 2), 3)
    pass_on(0)
    wait_bytes(v_share.at[0 : NB - 1, 0:NY], v_recv.at[2])
    for layer in range(CHUNK):
        v_buf[REACH + layer] = v_share[layer % NB, layer // NB]
    wait_bytes(o_home.at[0 : NY - 1], in_recv.at[1])
    for copy in o_halo(1):
        copy.start()

    def first_term(s, firsts):
        for first in firsts:
            u_buf[s, first : first + 8] = full_stencil(
                o_buf.at[s], first, v_buf[first : first + 8], first_scale, full_y, full_x
            )

    for s in range(NS):
        first_term(s, (12, 20))
    wait_bytes(v_share.at[0 : NB - 1, 0:2], v_recv.at[3])
    for layer in range(REACH):
        v_buf[layer] = v_share[NB - REACH + layer, NY]
        v_buf[REACH + CHUNK + layer] = v_share[layer, NY + 1]

    def share_layers(i, src, dst, s, send, recv):
        slot = ORB * band + NS * y + s
        for j in (3, 6, 1, 4, 7, 2, 5, 0):
            if i or j:
                remote(
                    src.at[y_layers[i] + band_ring[j]], dst.at[slot],
                    send.at[s], recv.at[s], {"band": band_ring[j], "dom": dom_ring[i]},
                ).start()
        if i == 0:
            dst[slot] = src[LAYERS * y + band]

    hear(0)
    pass_on(1)

    @pl.loop(0, NS)
    def _(s):
        for copy in o_halo(s):
            copy.wait_recv()
        first_term(s, (0, 4, 28, 36))
        for i in (1, 3, 2, 0):
            first = y_layers[i]
            value = full_stencil(
                u_buf.at[s], first, v_buf[pl.ds(REACH + first, 8)], second_scale, full_y, full_x
            )
            old = o_buf[s, pl.ds(2 * REACH + first, 8)]
            f_buf[s, pl.ds(REACH + first, 8)] = value - (first_ratio * second_ratio) * old
            share_layers(i, f_buf.at[s, REACH : REACH + CHUNK], f_all, s, f_send, f_recv)
        for copy in f_halo(s):
            copy.start()

    hear(1)
    pass_on(2)

    @pl.loop(0, NS)
    def _(s):
        for copy in f_halo(s):
            copy.wait_recv()
        for i in (1, 3, 2, 0):
            first = y_layers[i]
            g_buf[s, pl.ds(first, 8)] = half_stencil(
                f_buf.at[s], first, v_buf[pl.ds(REACH + first, 8)], half_y, half_x
            )
            share_layers(i, g_buf.at[s], g_all, s, g_send, g_recv)

    hear(2)

    def out_copy(s, peer):
        return remote(
            f_buf.at[s, pl.ds(REACH + LAYERS * peer, LAYERS)], f_ref.at[NS * y + s],
            out_send, out_recv, {"dom": z * NY + peer},
        )

    for s in range(NS):
        for peer in y_peers:
            out_copy(s, peer).start()
        f_ref[NS * y + s] = f_buf[s, pl.ds(REACH + LAYERS * y, LAYERS)]

    def pieces(rows, first, count, stride, c):
        value = jnp.concatenate(
            [rows[pl.ds(first + 2 * c + i, count, stride=stride), :] for i in range(2)], axis=1
        )
        return jnp.concatenate(split(value), axis=0)

    def against_f(left, c):
        return lax.dot_general(
            left, f_parts[c], (((1,), (1,)), ((), ())), preferred_element_type=f32
        )

    f_rows = f_all.reshape((NB * ORB + 2) * 16, 128)
    g_rows = g_all.reshape((NB * ORB + 2) * 16, 128)
    for s in range(NS):
        wait_bytes(f_all.at[0:PLANE], f_recv.at[s])
    total = jnp.zeros((128, 128), f32)
    for c in range(8):
        left = pieces(f_rows, 0, 64, 16, c)
        f_parts[c] = left
        total = total + against_f(left, c)
    lane = lax.broadcasted_iota(jnp.int32, (NB, 4, 128), 2)

    def band_tiles(value):
        value = value.reshape(NB, 8, 128)
        return jnp.where(lane < 64, value[:, 0:4], value[:, 4:8])

    def total_of(slots, count):
        total = slots[0]
        for i in range(1, count):
            total = total + slots[i]
        return total

    def over_band(tiles, slots, send, recv):
        for peer in band_peers:
            remote(tiles.at[peer], slots.at[band], send.at[0], recv.at[0], {"band": peer}).start()
        slots[band] = tiles[band]

    def over_dom(tiles, slots, send, recv):
        wait_bytes(tiles.at[0 : NB - 1], recv.at[0])
        slots[dom] = total_of(tiles, NB)
        for peer in dom_peers:
            remote(slots.at[dom], slots.at[dom], send.at[1], recv.at[1], {"dom": peer}).start()

    def result(slots, recv):
        wait_bytes(slots.at[0 : NY * NZ - 1], recv.at[1])
        return total_of(slots, NY * NZ) * (1.0 / TOTAL)

    margin = total[0:64] + total[64:128]
    m_part[...] = band_tiles(margin + pltpu.roll(margin, 64, 1))
    over_band(m_part, m_band, m_send, m_recv)
    for s in range(NS):
        wait_bytes(g_all.at[0:PLANE], g_recv.at[s])
        total = jnp.zeros((64, 128), f32)
        for c in range(8):
            total = total + against_f(pieces(g_rows, 16 * s, 32, 32, c), c)
        total = total[0:32] + total[32:64]
        y_rows[pl.ds(s, 32, stride=2), :] = total + pltpu.roll(total, 64, 1)
        if s == 0:
            over_dom(m_band, m_dom, m_send, m_recv)
    one_side = y_rows[0:64]
    other_side = jnp.concatenate([one_side, one_side], axis=0).T
    h_part[...] = band_tiles(one_side + other_side[0:64])
    over_band(h_part, h_band, r_send, r_recv)
    over_dom(h_band, h_dom, r_send, r_recv)
    margin = result(m_dom, m_recv)
    hamil = result(h_dom, r_recv)
    margin = jnp.concatenate([margin, pltpu.roll(margin, 64, 1)], axis=0)
    hamil = jnp.concatenate([pltpu.roll(hamil, 64, 1), hamil], axis=0)
    rows_ref[...] = jnp.where(lax.broadcasted_iota(jnp.int32, (8, 128), 1) < 64, margin, hamil)

    wait_bytes(o_home.at[0 : NS * (NY - 1)], out_recv)
    wait_bytes(o_home.at[0 : NS * (NY - 1)], out_send)
    wait_bytes(v_share.at[0, 0 : NY - 1], v_send.at[0])
    wait_bytes(v_share.at[0, 0:2], v_send.at[1])
    wait_bytes(v_share.at[0 : NB - 1, 0:NY], v_send.at[2])
    wait_bytes(v_share.at[0 : NB - 1, 0:2], v_send.at[3])

    @pl.loop(0, NS)
    def _(s):
        wait_bytes(o_home.at[0 : NY - 1], in_send.at[s])
        for copy in o_halo(s) + f_halo(s):
            copy.wait_send()
        wait_bytes(f_all.at[0:PLANE], f_send.at[s])
        wait_bytes(g_all.at[0:PLANE], g_send.at[s])

    for send in (m_send, r_send):
        wait_bytes(h_dom.at[0 : NB - 1], send.at[0])
        wait_bytes(h_dom.at[0 : NY * NZ - 1], send.at[1])


def finish(f_ref, rows_ref, out_hbm, ham_hbm, mar_hbm, ham, mar, sems):
    copies = [
        pltpu.make_async_copy(f_ref.at[2 * i : 2 * i + 2], out_hbm.at[2 * i : 2 * i + 2], sems.at[i])
        for i in range(4)
    ]
    copies.append(pltpu.make_async_copy(ham, ham_hbm, sems.at[4]))
    copies.append(pltpu.make_async_copy(mar, mar_hbm, sems.at[5]))
    for copy in copies[:4]:
        copy.start()
    ham[...] = rows_ref[:, 64:128]
    mar[...] = rows_ref[:, 0:64]
    for copy in copies[4:]:
        copy.start()
    for copy in copies:
        copy.wait()


def on_device(orbitals, potential):
    dma = pltpu.SemaphoreType.DMA
    in_hbm = pl.BlockSpec(memory_space=pltpu.HBM)
    in_vmem = pl.BlockSpec(memory_space=pltpu.VMEM)
    matrices = [jnp.asarray(m) for both in (True, False) for m in in_plane_matrices(both)]
    filtered, rows = pl.pallas_call(
        kernel,
        out_shape=(
            pltpu.VMEM((ORB, LAYERS, 16, 128), f32),
            pltpu.VMEM((8, 128), f32),
        ),
        in_specs=[in_hbm] * 6,
        out_specs=(in_vmem, in_vmem),
        scratch_shapes=[
            pltpu.VMEM((256, 256), bf16),
            pltpu.VMEM((128, 384), bf16),
            pltpu.VMEM((256, 256), bf16),
            pltpu.VMEM((128, 384), bf16),
            pltpu.VMEM((ORB, LAYERS, 16, 128), f32),
            pltpu.VMEM((NB, NY + 2, 16, 128), f32),
            pltpu.VMEM((CHUNK + 2 * REACH, 16, 128), f32),
            pltpu.VMEM((NS, CHUNK + 4 * REACH, 16, 128), f32),
            pltpu.VMEM((NS, CHUNK + 2 * REACH, 16, 128), f32),
            pltpu.VMEM((NS, CHUNK + 2 * REACH, 16, 128), f32),
            pltpu.VMEM((NS, CHUNK, 16, 128), f32),
            pltpu.VMEM((NB * ORB + 2, 16, 128), f32),
            pltpu.VMEM((NB * ORB + 2, 16, 128), f32),
            pltpu.VMEM((8, 128, 256), bf16),
            pltpu.VMEM((72, 128), f32),
            pltpu.VMEM((NB, 4, 128), f32),
            pltpu.VMEM((NB, 4, 128), f32),
            pltpu.VMEM((NY * NZ, 4, 128), f32),
            pltpu.VMEM((NB, 4, 128), f32),
            pltpu.VMEM((NB, 4, 128), f32),
            pltpu.VMEM((NY * NZ, 4, 128), f32),
            dma((7,)),
            dma((NS,)), dma((NS,)),
            dma((4,)), dma((4,)),
            dma((NS, 2)), dma((NS, 2)),
            dma((NS, 2)), dma((NS, 2)),
            dma((NS,)), dma((NS,)), dma((NS,)), dma((NS,)),
            dma, dma, dma((2,)), dma((2,)), dma((2,)), dma((2,)),
            pltpu.SemaphoreType.REGULAR((3, 2)),
        ],
        compiler_params=pltpu.CompilerParams(
            collective_id=0, has_side_effects=True, vmem_limit_bytes=60 * 1024 * 1024
        ),
    )(orbitals, potential, *matrices)
    return pl.pallas_call(
        finish,
        out_shape=(
            jax.ShapeDtypeStruct((ORB, LAYERS, 16, 128), f32),
            jax.ShapeDtypeStruct((8, 64), f32),
            jax.ShapeDtypeStruct((8, 64), f32),
        ),
        in_specs=[in_vmem, in_vmem],
        out_specs=(in_hbm, in_hbm, in_hbm),
        scratch_shapes=[pltpu.VMEM((8, 64), f32), pltpu.VMEM((8, 64), f32), dma((6,))],
        compiler_params=pltpu.CompilerParams(vmem_limit_bytes=16 * 1024 * 1024),
    )(filtered, rows)


def solution(mesh):
    in_specs = (P("band", "dom", None, None), P("dom", None, None))
    out_specs = (P("band", "dom", None, None), P("band", None), P("band", None))
    return jax.shard_map(
        on_device, mesh=mesh, in_specs=in_specs, out_specs=out_specs, check_vma=False
    )
```

```python
import jax
import jax.numpy as jnp
import ml_dtypes
import numpy as np
from jax import lax
from jax.experimental import pallas as pl
from jax.experimental.pallas import tpu as pltpu
from jax.sharding import PartitionSpec as P

MESH = pl.DeviceIdType.MESH

stencil_weights = (
    -5369.0 / 1800.0,
    12.0 / 7.0,
    -15.0 / 56.0,
    10.0 / 189.0,
    -1.0 / 112.0,
    2.0 / 825.0,
    -1.0 / 2772.0,
)
spacing = 0.35
kinetic = -0.5 / (spacing * spacing)
upper_bound = 90.0
cutoff = 8.0
lower_bound = -11.0
center = (upper_bound + cutoff) / 2.0
half_width = (upper_bound - cutoff) / 2.0
first_ratio = half_width / (lower_bound - center)
second_ratio = 1.0 / (2.0 / first_ratio - first_ratio)
first_scale = first_ratio / half_width
second_scale = 2.0 * second_ratio / half_width

NB = 8
NY = 4
NZ = 8
ORB = 8
NS = ORB // NY
LAYERS = 8
CHUNK = NY * LAYERS
REACH = 6
PLANE = NB * NY - 1
TOTAL = 256 * 16 * 128
bf16 = jnp.bfloat16
f32 = jnp.float32


def in_plane_matrices(both_sides):
    def circulant(n):
        shift = (np.arange(n)[:, None] - np.arange(n)[None, :]) % n
        matrix = np.zeros((n, n))
        for o in range(1, REACH + 1):
            matrix += stencil_weights[o] * (shift == o)
            if both_sides:
                matrix += stencil_weights[o] * (shift == n - o)
        return matrix

    def parts(matrix):
        matrix = matrix.astype(np.float32)
        high = matrix.astype(ml_dtypes.bfloat16)
        return high, (matrix - high.astype(np.float32)).astype(ml_dtypes.bfloat16)

    y_high, y_low = parts(circulant(128))
    x_high, x_low = parts(np.kron(np.eye(8), circulant(16)))
    along_y = np.block([[y_high, y_low], [y_high, np.zeros_like(y_low)]])
    return along_y, np.concatenate([x_high, x_high, x_low], axis=1)


def split(value):
    high = value.astype(bf16)
    return high, (value - high.astype(f32)).astype(bf16)


def in_plane(mid, along_y, along_x):
    high, low = split(mid.reshape(8 * 16, 128))
    y_sum = jnp.dot(jnp.concatenate([high, low], axis=1), along_y[...], preferred_element_type=f32)
    x_sum = jnp.dot(
        along_x[...], jnp.concatenate([high, low, high], axis=0), preferred_element_type=f32
    )
    return (y_sum[:, :128] + y_sum[:, 128:] + x_sum).reshape(8, 16, 128)


def full_stencil(src, first, potential, scale, along_y, along_x):
    layer = [src[first + z] for z in range(8 + 2 * REACH)]
    mid = jnp.stack(layer[REACH : REACH + 8])
    normal = []
    for z in range(REACH, REACH + 8):
        total = stencil_weights[1] * (layer[z + 1] + layer[z - 1])
        for o in range(2, REACH + 1):
            total = total + stencil_weights[o] * (layer[z + o] + layer[z - o])
        normal.append(total)
    sums = jnp.stack(normal) + in_plane(mid, along_y, along_x)
    diagonal = scale * (potential + (3.0 * kinetic * stencil_weights[0] - center))
    return (scale * kinetic) * sums + diagonal * mid


def half_stencil(src, first, potential, along_y, along_x):
    mid = src[pl.ds(first + REACH, 8)]
    above = [src[first + REACH + z, 0:8] for z in range(8 + REACH)]
    below = [src[first + z, 8:16] for z in range(8 + REACH)]
    normal = []
    for z in range(8):
        up = stencil_weights[1] * above[z + 1]
        down = stencil_weights[1] * below[z + REACH - 1]
        for o in range(2, REACH + 1):
            up = up + stencil_weights[o] * above[z + o]
            down = down + stencil_weights[o] * below[z + REACH - o]
        normal.append(jnp.concatenate([up, down], axis=0))
    sums = jnp.stack(normal) + in_plane(mid, along_y, along_x)
    return kinetic * sums + (0.5 * potential + 1.5 * kinetic * stencil_weights[0]) * mid


def kernel(
    orb_hbm, pot_hbm, mats_hbm0, mats_hbm1, mats_hbm2, mats_hbm3, f_ref, rows_ref,
    full_y, full_x, half_y, half_x,
    o_home, v_share, v_buf, o_buf, u_buf, f_buf, g_buf, f_all, g_all, f_parts, y_rows,
    m_part, m_band, m_dom, h_part, h_band, h_dom,
    load_sem, in_send, in_recv, v_send, v_recv, z_send, z_recv, h_send, h_recv,
    f_send, f_recv, g_send, g_recv, out_send, out_recv, m_send, m_recv, r_send, r_recv, relay,
):
    band = lax.axis_index("band")
    dom = lax.axis_index("dom")
    y = lax.rem(dom, NY)
    z = lax.div(dom, NY)
    z_up = lax.rem(z + 1, NZ) * NY + y
    z_down = lax.rem(z + NZ - 1, NZ) * NY + y
    y_peers = [lax.rem(y + j, NY) for j in (1, 3, 2)]
    band_peers = [lax.rem(band + j, NB) for j in (4, 3, 5, 2, 6, 1, 7)]

    barrier = pltpu.get_barrier_semaphore()
    for peer in [z_up, z_down] + [z * NY + peer for peer in y_peers]:
        pl.semaphore_signal(barrier, inc=1, device_id={"dom": peer}, device_id_type=MESH)
    for peer in band_peers:
        pl.semaphore_signal(barrier, inc=1, device_id={"band": peer}, device_id_type=MESH)

    loads = [
        pltpu.make_async_copy(orb_hbm, o_home, load_sem.at[0]),
        pltpu.make_async_copy(pot_hbm.at[band], v_share.at[band, y], load_sem.at[1]),
        pltpu.make_async_copy(mats_hbm0, full_y, load_sem.at[2]),
        pltpu.make_async_copy(mats_hbm1, full_x, load_sem.at[3]),
        pltpu.make_async_copy(mats_hbm2, half_y, load_sem.at[4]),
        pltpu.make_async_copy(mats_hbm3, half_x, load_sem.at[5]),
        pltpu.make_async_copy(
            orb_hbm.at[pl.ds(NS * y, NS)],
            o_buf.at[:, pl.ds(2 * REACH + LAYERS * y, LAYERS)],
            load_sem.at[6],
        ),
    ]
    for load in loads:
        load.start()
    z_rows = [lax.rem(z + j, NZ) * NY for j in range(NZ)]
    y_columns = [lax.rem(y + j, NY) for j in range(NY)]
    offsets = [(i, j) for i in range(NZ) for j in range(NY) if i or j]
    offsets.sort(key=lambda ij: -min(ij[0], NZ - ij[0]) - min(ij[1], NY - ij[1]))
    dom_peers = [z_rows[i] + y_columns[j] for i, j in offsets]

    band_ring = [lax.rem(band + j, NB) for j in range(NB)]
    y_layers = [LAYERS * lax.rem(y + i, NY) for i in range(NY)]
    dom_ring = [z * NY + lax.rem(y + i, NY) for i in range(NY)]

    for load in loads:
        load.wait()
    pl.semaphore_wait(barrier, 2 + (NY - 1) + (NB - 1))

    def remote(src, dst, send, recv, where):
        return pltpu.make_async_remote_copy(
            src_ref=src, dst_ref=dst, send_sem=send, recv_sem=recv,
            device_id=where, device_id_type=MESH,
        )

    def wait_bytes(ref, sem):
        pltpu.make_async_copy(ref, ref, sem).wait()

    def in_copy(s, peer):
        return remote(
            o_home.at[NS * peer + s], o_buf.at[s, pl.ds(2 * REACH + LAYERS * y, LAYERS)],
            in_send.at[s], in_recv.at[s], {"dom": z * NY + peer},
        )

    def z_copies(src, width, send, recv):
        low, high = src.shape[0] - width, src.shape[0] - 2 * width
        return (
            remote(src.at[high:low], src.at[0:width], send.at[0], recv.at[0], {"dom": z_up}),
            remote(src.at[width : 2 * width], src.at[low:], send.at[1], recv.at[1], {"dom": z_down}),
        )

    def o_halo(s):
        return z_copies(o_buf.at[s], 2 * REACH, z_send.at[s], z_recv.at[s])

    def f_halo(s):
        src = f_buf.at[s]
        return (
            remote(
                src.at[CHUNK : CHUNK + REACH, 8:16], src.at[0:REACH, 8:16],
                h_send.at[s, 0], h_recv.at[s, 0], {"dom": z_up},
            ),
            remote(
                src.at[REACH : 2 * REACH, 0:8], src.at[CHUNK + REACH :, 0:8],
                h_send.at[s, 1], h_recv.at[s, 1], {"dom": z_down},
            ),
        )

    def pass_on(i):
        pl.semaphore_signal(relay.at[i, 0], inc=1, device_id={"dom": z_up}, device_id_type=MESH)
        pl.semaphore_signal(relay.at[i, 1], inc=1, device_id={"dom": z_down}, device_id_type=MESH)

    def hear(i):
        for j in range(2):
            pl.semaphore_wait(relay.at[i, j], 1)

    def v_round(slots, i):
        for peer in band_peers:
            src = v_share.at[band, slots]
            remote(src, src, v_send.at[i], v_recv.at[i], {"band": peer}).start()

    for peer in y_peers:
        src = v_share.at[band, y]
        remote(src, src, v_send.at[0], v_recv.at[0], {"dom": z * NY + peer}).start()
    for peer in y_peers:
        in_copy(0, peer).start()
    wait_bytes(v_share.at[0, 0 : NY - 1], v_recv.at[0])
    for peer in y_peers:
        in_copy(1, peer).start()
    remote(
        v_share.at[band, NY - 1], v_share.at[band, NY], v_send.at[1], v_recv.at[1], {"dom": z_up}
    ).start()
    remote(
        v_share.at[band, 0], v_share.at[band, NY + 1], v_send.at[1], v_recv.at[1], {"dom": z_down}
    ).start()
    v_round(slice(0, NY), 2)
    wait_bytes(o_home.at[0 : NY - 1], in_recv.at[0])
    for copy in o_halo(0):
        copy.start()
    wait_bytes(v_share.at[0, 0:2], v_recv.at[1])
    v_round(slice(NY, NY + 2), 3)
    pass_on(0)
    wait_bytes(v_share.at[0 : NB - 1, 0:NY], v_recv.at[2])
    for layer in range(CHUNK):
        v_buf[REACH + layer] = v_share[layer % NB, layer // NB]
    wait_bytes(o_home.at[0 : NY - 1], in_recv.at[1])
    for copy in o_halo(1):
        copy.start()

    def first_term(s, firsts):
        for first in firsts:
            u_buf[s, first : first + 8] = full_stencil(
                o_buf.at[s], first, v_buf[first : first + 8], first_scale, full_y, full_x
            )

    for s in range(NS):
        first_term(s, (12, 20))
    wait_bytes(v_share.at[0 : NB - 1, 0:2], v_recv.at[3])
    for layer in range(REACH):
        v_buf[layer] = v_share[NB - REACH + layer, NY]
        v_buf[REACH + CHUNK + layer] = v_share[layer, NY + 1]

    def share_layers(i, src, dst, s, send, recv):
        slot = ORB * band + NS * y + s
        for j in (3, 6, 1, 4, 7, 2, 5, 0):
            if i or j:
                remote(
                    src.at[y_layers[i] + band_ring[j]], dst.at[slot],
                    send.at[s], recv.at[s], {"band": band_ring[j], "dom": dom_ring[i]},
                ).start()
        if i == 0:
            dst[slot] = src[LAYERS * y + band]

    hear(0)
    pass_on(1)

    @pl.loop(0, NS)
    def _(s):
        for copy in o_halo(s):
            copy.wait_recv()
        first_term(s, (0, 4, 28, 36))
        for i in (1, 3, 2, 0):
            first = y_layers[i]
            value = full_stencil(
                u_buf.at[s], first, v_buf[pl.ds(REACH + first, 8)], second_scale, full_y, full_x
            )
            old = o_buf[s, pl.ds(2 * REACH + first, 8)]
            f_buf[s, pl.ds(REACH + first, 8)] = value - (first_ratio * second_ratio) * old
            if i in (1, 3):
                share_layers(i, f_buf.at[s, REACH : REACH + CHUNK], f_all, s, f_send, f_recv)
        for copy in f_halo(s):
            copy.start()
        for i in (2, 0):
            share_layers(i, f_buf.at[s, REACH : REACH + CHUNK], f_all, s, f_send, f_recv)

    hear(1)
    pass_on(2)

    @pl.loop(0, NS)
    def _(s):
        for copy in f_halo(s):
            copy.wait_recv()
        for i in (1, 3, 2, 0):
            first = y_layers[i]
            g_buf[s, pl.ds(first, 8)] = half_stencil(
                f_buf.at[s], first, v_buf[pl.ds(REACH + first, 8)], half_y, half_x
            )
            share_layers(i, g_buf.at[s], g_all, s, g_send, g_recv)

    hear(2)

    def out_copy(s, peer):
        return remote(
            f_buf.at[s, pl.ds(REACH + LAYERS * peer, LAYERS)], f_ref.at[NS * y + s],
            out_send, out_recv, {"dom": z * NY + peer},
        )

    for s in range(NS):
        for peer in y_peers:
            out_copy(s, peer).start()
        f_ref[NS * y + s] = f_buf[s, pl.ds(REACH + LAYERS * y, LAYERS)]

    def pieces(rows, first, count, stride, c):
        value = jnp.concatenate(
            [rows[pl.ds(first + 2 * c + i, count, stride=stride), :] for i in range(2)], axis=1
        )
        return jnp.concatenate(split(value), axis=0)

    def against_f(left, c):
        return lax.dot_general(
            left, f_parts[c], (((1,), (1,)), ((), ())), preferred_element_type=f32
        )

    f_rows = f_all.reshape((NB * ORB + 2) * 16, 128)
    g_rows = g_all.reshape((NB * ORB + 2) * 16, 128)
    for s in range(NS):
        wait_bytes(f_all.at[0:PLANE], f_recv.at[s])
    total = jnp.zeros((128, 128), f32)
    for c in range(8):
        left = pieces(f_rows, 0, 64, 16, c)
        f_parts[c] = left
        total = total + against_f(left, c)
    lane = lax.broadcasted_iota(jnp.int32, (NB, 4, 128), 2)

    def band_tiles(value):
        value = value.reshape(NB, 8, 128)
        return jnp.where(lane < 64, value[:, 0:4], value[:, 4:8])

    def total_of(slots, count):
        total = slots[0]
        for i in range(1, count):
            total = total + slots[i]
        return total

    def over_band(tiles, slots, send, recv):
        for peer in band_peers:
            remote(tiles.at[peer], slots.at[band], send.at[0], recv.at[0], {"band": peer}).start()
        slots[band] = tiles[band]

    def over_dom(tiles, slots, send, recv):
        wait_bytes(tiles.at[0 : NB - 1], recv.at[0])
        slots[dom] = total_of(tiles, NB)
        for peer in dom_peers:
            remote(slots.at[dom], slots.at[dom], send.at[1], recv.at[1], {"dom": peer}).start()

    def result(slots, recv):
        wait_bytes(slots.at[0 : NY * NZ - 1], recv.at[1])
        return total_of(slots, NY * NZ) * (1.0 / TOTAL)

    margin = total[0:64] + total[64:128]
    m_part[...] = band_tiles(margin + pltpu.roll(margin, 64, 1))
    over_band(m_part, m_band, m_send, m_recv)
    for s in range(NS):
        wait_bytes(g_all.at[0:PLANE], g_recv.at[s])
        total = jnp.zeros((64, 128), f32)
        for c in range(8):
            total = total + against_f(pieces(g_rows, 16 * s, 32, 32, c), c)
        total = total[0:32] + total[32:64]
        y_rows[pl.ds(s, 32, stride=2), :] = total + pltpu.roll(total, 64, 1)
        if s == 0:
            over_dom(m_band, m_dom, m_send, m_recv)
    one_side = y_rows[0:64]
    other_side = jnp.concatenate([one_side, one_side], axis=0).T
    h_part[...] = band_tiles(one_side + other_side[0:64])
    over_band(h_part, h_band, r_send, r_recv)
    over_dom(h_band, h_dom, r_send, r_recv)
    margin = result(m_dom, m_recv)
    hamil = result(h_dom, r_recv)
    margin = jnp.concatenate([margin, pltpu.roll(margin, 64, 1)], axis=0)
    hamil = jnp.concatenate([pltpu.roll(hamil, 64, 1), hamil], axis=0)
    rows_ref[...] = jnp.where(lax.broadcasted_iota(jnp.int32, (8, 128), 1) < 64, margin, hamil)

    wait_bytes(o_home.at[0 : NS * (NY - 1)], out_recv)
    wait_bytes(o_home.at[0 : NS * (NY - 1)], out_send)
    wait_bytes(v_share.at[0, 0 : NY - 1], v_send.at[0])
    wait_bytes(v_share.at[0, 0:2], v_send.at[1])
    wait_bytes(v_share.at[0 : NB - 1, 0:NY], v_send.at[2])
    wait_bytes(v_share.at[0 : NB - 1, 0:2], v_send.at[3])

    @pl.loop(0, NS)
    def _(s):
        wait_bytes(o_home.at[0 : NY - 1], in_send.at[s])
        for copy in o_halo(s) + f_halo(s):
            copy.wait_send()
        wait_bytes(f_all.at[0:PLANE], f_send.at[s])
        wait_bytes(g_all.at[0:PLANE], g_send.at[s])

    for send in (m_send, r_send):
        wait_bytes(h_dom.at[0 : NB - 1], send.at[0])
        wait_bytes(h_dom.at[0 : NY * NZ - 1], send.at[1])


def finish(f_ref, rows_ref, out_hbm, ham_hbm, mar_hbm, ham, mar, sems):
    copies = [
        pltpu.make_async_copy(f_ref.at[2 * i : 2 * i + 2], out_hbm.at[2 * i : 2 * i + 2], sems.at[i])
        for i in range(4)
    ]
    copies.append(pltpu.make_async_copy(ham, ham_hbm, sems.at[4]))
    copies.append(pltpu.make_async_copy(mar, mar_hbm, sems.at[5]))
    for copy in copies[:4]:
        copy.start()
    ham[...] = rows_ref[:, 64:128]
    mar[...] = rows_ref[:, 0:64]
    for copy in copies[4:]:
        copy.start()
    for copy in copies:
        copy.wait()


def on_device(orbitals, potential):
    dma = pltpu.SemaphoreType.DMA
    in_hbm = pl.BlockSpec(memory_space=pltpu.HBM)
    in_vmem = pl.BlockSpec(memory_space=pltpu.VMEM)
    matrices = [jnp.asarray(m) for both in (True, False) for m in in_plane_matrices(both)]
    filtered, rows = pl.pallas_call(
        kernel,
        out_shape=(
            pltpu.VMEM((ORB, LAYERS, 16, 128), f32),
            pltpu.VMEM((8, 128), f32),
        ),
        in_specs=[in_hbm] * 6,
        out_specs=(in_vmem, in_vmem),
        scratch_shapes=[
            pltpu.VMEM((256, 256), bf16),
            pltpu.VMEM((128, 384), bf16),
            pltpu.VMEM((256, 256), bf16),
            pltpu.VMEM((128, 384), bf16),
            pltpu.VMEM((ORB, LAYERS, 16, 128), f32),
            pltpu.VMEM((NB, NY + 2, 16, 128), f32),
            pltpu.VMEM((CHUNK + 2 * REACH, 16, 128), f32),
            pltpu.VMEM((NS, CHUNK + 4 * REACH, 16, 128), f32),
            pltpu.VMEM((NS, CHUNK + 2 * REACH, 16, 128), f32),
            pltpu.VMEM((NS, CHUNK + 2 * REACH, 16, 128), f32),
            pltpu.VMEM((NS, CHUNK, 16, 128), f32),
            pltpu.VMEM((NB * ORB + 2, 16, 128), f32),
            pltpu.VMEM((NB * ORB + 2, 16, 128), f32),
            pltpu.VMEM((8, 128, 256), bf16),
            pltpu.VMEM((72, 128), f32),
            pltpu.VMEM((NB, 4, 128), f32),
            pltpu.VMEM((NB, 4, 128), f32),
            pltpu.VMEM((NY * NZ, 4, 128), f32),
            pltpu.VMEM((NB, 4, 128), f32),
            pltpu.VMEM((NB, 4, 128), f32),
            pltpu.VMEM((NY * NZ, 4, 128), f32),
            dma((7,)),
            dma((NS,)), dma((NS,)),
            dma((4,)), dma((4,)),
            dma((NS, 2)), dma((NS, 2)),
            dma((NS, 2)), dma((NS, 2)),
            dma((NS,)), dma((NS,)), dma((NS,)), dma((NS,)),
            dma, dma, dma((2,)), dma((2,)), dma((2,)), dma((2,)),
            pltpu.SemaphoreType.REGULAR((3, 2)),
        ],
        compiler_params=pltpu.CompilerParams(
            collective_id=0, has_side_effects=True, vmem_limit_bytes=60 * 1024 * 1024
        ),
    )(orbitals, potential, *matrices)
    return pl.pallas_call(
        finish,
        out_shape=(
            jax.ShapeDtypeStruct((ORB, LAYERS, 16, 128), f32),
            jax.ShapeDtypeStruct((8, 64), f32),
            jax.ShapeDtypeStruct((8, 64), f32),
        ),
        in_specs=[in_vmem, in_vmem],
        out_specs=(in_hbm, in_hbm, in_hbm),
        scratch_shapes=[pltpu.VMEM((8, 64), f32), pltpu.VMEM((8, 64), f32), dma((6,))],
        compiler_params=pltpu.CompilerParams(vmem_limit_bytes=16 * 1024 * 1024),
    )(filtered, rows)


def solution(mesh):
    in_specs = (P("band", "dom", None, None), P("dom", None, None))
    out_specs = (P("band", "dom", None, None), P("band", None), P("band", None))
    return jax.shard_map(
        on_device, mesh=mesh, in_specs=in_specs, out_specs=out_specs, check_vma=False
    )
```
